32 devices in a mesh: ctx: 16 (over z, y, core), ch: 2 (over x).
Axes of the slice: x: 2, y: 2, z: 4, core: 2. Of those that a mesh axis runs over, the one named last changes fastest.
Arguments:
- cotangent: bfloat16 [2048, 4096], P('ctx', 'ch'), may hold values from -6 to 6
- out_weight: bfloat16 [4096, 4096], P('ch', 'ctx'), may hold values from -0.09375 to 0.09375
- gate_value: float32 [2048, 4096], P('ctx', 'ch'), may hold values from -6 to 6
- conv_output: float32 [2048, 4096], P('ctx', 'ch'), may hold values from -6 to 6
- conv_input: float32 [2048, 4096], P('ctx', 'ch'), may hold values from -6 to 6
- filters: float32 [256, 2048], P('ch'), may hold values from -1 to 1
Outputs:
- input_grad: float32 [2048, 4096], P('ctx', 'ch')
- gate_grad: float32 [2048, 4096], P('ctx', 'ch')
- filter_grad: float32 [256, 2048], P('ch', 'ctx')
The draws below stay inside these ranges and needn't reach their ends.
All inputs are finite; a program needn't handle non-finite values.
Results may differ from the reference program's by a relative error of at most 0.0003.
Values may be sent and summed in bfloat16 or wider, within the bound.
No kernel may reach another device: no remote copies, remote signals or barrier semaphores. Data moves between devices by JAX's collectives and lax.ppermute only.
A program may use at most 128 MiB of HBM per device.

```python
import math
import jax
import jax.numpy as jnp
from jax import lax

TOK_DEV = 128
GROUPS = 256
GROUP_CH = 16
LAGS = 2048
D = 4096
TOKENS = 2048


def draw_filters(key, part):
    subkeys = jax.random.split(jax.random.fold_in(key, 7), 6)
    positions = jnp.arange(LAGS).astype(jnp.float32)
    fast_limit = 5
    slow_low = 1.0
    slow_high = 6.0
    fast_group = jax.random.randint(subkeys[0], (GROUPS, 1), 0, 10) < fast_limit
    slow_decay = LAGS * jnp.exp(jax.random.uniform(subkeys[1], (GROUPS, 1), minval=math.log(slow_low), maxval=math.log(slow_high)))
    fast_decay = TOK_DEV * jax.random.uniform(subkeys[2], (GROUPS, 1), minval=0.25, maxval=0.4)
    decay = jnp.where(fast_group, fast_decay, slow_decay)
    envelope = jnp.exp(-positions[None, :] / decay)
    spots = jax.random.randint(subkeys[3], (GROUPS, 2, 1), 1, LAGS)
    drops = jax.random.uniform(subkeys[4], (GROUPS, 2, 1), minval=0.6, maxval=0.8)
    envelope = envelope * jnp.prod(jnp.where(positions[None, None, :] >= spots.astype(jnp.float32), drops, 1.0), axis=1)
    raw_taps = jax.random.normal(subkeys[5], (GROUPS, LAGS)) * envelope
    return raw_taps / jnp.sqrt(jnp.sum(raw_taps * raw_taps, axis=1, keepdims=True))


def block_levels(rng, dims, pieces, low, largest):
    factor_of, own = 1.0, jax.random.fold_in(rng, 6)
    for position, blocks in pieces:
        draws = jnp.exp(jax.random.uniform(jax.random.fold_in(own, position), (blocks,), jnp.float32, low / len(pieces), largest / len(pieces)))
        factor_of = factor_of * jnp.repeat(draws, dims[position] // blocks).reshape([-1 if axis == position else 1 for axis in range(len(dims))])
    return factor_of


def gaussian(rng, shape, spread, most, cuts=(), dtype=jnp.bfloat16):
    drawn = spread * jax.random.normal(rng, shape, jnp.float32)
    if cuts:
        drawn = drawn * block_levels(rng, shape, cuts, -0.22, 0.18)
    return jnp.clip(drawn, -most, most).astype(dtype)


def setup_inputs(seed: int = 0) -> dict:
    key_of = jax.random.split(jax.random.key(seed), 7)
    cotangent = gaussian(key_of[0], (TOKENS, D), 1.0, 6.0, ((0, 16), (1, 2)))
    out_weight = gaussian(key_of[1], (D, D), D ** -0.5, 0.09375, ((0, 2), (1, 16)))
    gate_value = gaussian(key_of[2], (TOKENS, D), 1.0, 6.0, ((0, 16), (1, 2)), jnp.float32)
    conv_output = gaussian(key_of[3], (TOKENS, D), 1.0, 6.0, ((0, 16), (1, 2)), jnp.float32)
    conv_input = gaussian(key_of[4], (TOKENS, D), 1.0, 6.0, ((0, 16), (1, 2)), jnp.float32)
    filters = draw_filters(jax.random.fold_in(key_of[6], 71), 0)
    return {"cotangent": cotangent, "out_weight": out_weight, "gate_value": gate_value, "conv_output": conv_output, "conv_input": conv_input, "filters": filters}


def reference(cotangent, out_weight, gate_value, conv_output, conv_input, filters):
    grad_out = jnp.dot(cotangent, out_weight.T, preferred_element_type=jnp.float32)
    gate_grad = grad_out * conv_output
    seq_grad = grad_out * gate_value
    fft_length = TOKENS + LAGS
    group_batch = math.gcd(GROUPS, 16)
    batch_count = GROUPS // group_batch
    width = group_batch * GROUP_CH
    grad_blocks = seq_grad.reshape(TOKENS, batch_count, width).transpose(1, 0, 2)
    input_blocks = conv_input.reshape(TOKENS, batch_count, width).transpose(1, 0, 2)
    filter_blocks = filters.reshape(batch_count, group_batch, LAGS)

    def per_block(operands):
        grad_rows, input_rows, filter_rows = operands
        grad_spectrum = jnp.fft.rfft(grad_rows, n=fft_length, axis=0)
        input_spectrum = jnp.fft.rfft(input_rows, n=fft_length, axis=0)
        filter_spectrum = jnp.fft.rfft(filter_rows, n=fft_length, axis=1)
        channel_spectrum = jnp.repeat(filter_spectrum.T, GROUP_CH, axis=1)
        input_part = jnp.fft.irfft(grad_spectrum * jnp.conj(channel_spectrum), n=fft_length, axis=0)[:TOKENS]
        cross_spectrum = (grad_spectrum * jnp.conj(input_spectrum)).reshape(-1, group_batch, GROUP_CH).sum(axis=2)
        lag_part = jnp.fft.irfft(cross_spectrum, n=fft_length, axis=0)[:LAGS].T
        return (input_part.astype(jnp.float32), lag_part.astype(jnp.float32))
    input_parts, lag_parts = lax.map(per_block, (grad_blocks, input_blocks, filter_blocks))
    input_grad = input_parts.transpose(1, 0, 2).reshape(TOKENS, D)
    filter_grad = lag_parts.reshape(GROUPS, LAGS) * (1.0 / math.sqrt(GROUP_CH * TOKENS))
    return (input_grad, gate_grad, filter_grad)
```

```python
import functools
import math

import jax
import jax.numpy as jnp
from jax import lax
from jax.experimental import pallas as pl
from jax.experimental.pallas import tpu as pltpu
from jax.sharding import PartitionSpec as P

LANES = 128
ROW_TILE = 16
VMEM = pl.BlockSpec(memory_space=pltpu.VMEM)


def split(value):
    high = value.astype(jnp.bfloat16)
    return high, (value - high.astype(jnp.float32)).astype(jnp.bfloat16)


def toeplitz_kernel(filter_ref, out_ref):
    tok = out_ref.shape[1] // 2
    rows = jnp.broadcast_to(filter_ref[0], (tok, filter_ref.shape[2]))
    high, low = split(pltpu.roll(rows, 0, 1, stride=1, stride_axis=0))
    out_ref[0, :tok, :] = high
    out_ref[0, tok:, :] = low


def toeplitz(filters, tok):
    groups, lags = filters.shape
    width = lags + tok
    padded = jnp.pad(filters, ((0, 0), (0, tok)))[:, None, :]
    return pl.pallas_call(
        toeplitz_kernel,
        grid=(groups,),
        in_specs=[pl.BlockSpec((1, 1, width), lambda g: (g, 0, 0))],
        out_specs=pl.BlockSpec((1, 2 * tok, width), lambda g: (g, 0, 0)),
        out_shape=jax.ShapeDtypeStruct((groups, 2 * tok, width), jnp.bfloat16),
        cost_estimate=pl.CostEstimate(
            flops=groups * tok * width * 4, bytes_accessed=groups * width * (4 + 4 * tok), transcendentals=0
        ),
        name="toeplitz",
    )(padded)


def conv_kernel(
    scale, lag_own, s_ref, x_ref, t_ref, out_ref, s_hi, s_lo, x_hi, x_lo, total, grads, cross, lag_sums
):
    blocks, tok, _ = s_ref.shape
    groups, rows, _ = x_hi.shape
    per = rows // blocks
    width = t_ref.shape[2]
    steps = width // tok
    used = min(steps, blocks)
    s_hi[:, rows:, :] = jnp.zeros_like(s_hi[:, rows:, :])
    s_lo[:, rows:, :] = jnp.zeros_like(s_lo[:, rows:, :])

    @pl.loop(0, blocks)
    def _(a):
        at = pl.ds(pl.multiple_of(a * per, per), per)
        for source, high_ref, low_ref in ((s_ref, s_hi, s_lo), (x_ref, x_hi, x_lo)):
            high, low = split(source[a].T[: groups * per])
            high_ref[:, at, :] = high.reshape(groups, per, tok)
            low_ref[:, at, :] = low.reshape(groups, per, tok)

    @pl.loop(0, groups)
    def _(g):
        for d in range(0, used, 2):
            first, second = d * per, (d + 1) * per
            count = rows - first
            left = jnp.concatenate(
                [
                    jnp.concatenate([ref[g, first : first + count, :], ref[g, second : second + count, :]], axis=1)
                    for ref in (s_hi, s_lo)
                ],
                axis=0,
            )
            if d + 2 <= steps:
                right = t_ref[g, :, d * tok : (d + 2) * tok]
            else:
                right = jnp.concatenate(
                    [t_ref[g, :, d * tok :], jnp.zeros((2 * tok, tok), jnp.bfloat16)], axis=1
                )
            product = lax.dot_general(
                left, right, (((1,), (1,)), ((), ())), preferred_element_type=jnp.float32
            )
            term = product[:count, :tok] + (product[:count, tok:] + product[count:, :tok])
            if d == 0:
                total[...] = term
            else:
                total[:count, :] += term
        grads[g] = total[...]

        left = jnp.concatenate([x_hi[g], x_lo[g]], axis=1).T
        for d in range(used):
            here = pl.ds(d * per, rows)
            right = jnp.concatenate([s_hi[g, here, :], s_lo[g, here, :]], axis=1)
            product = jnp.dot(left, right, preferred_element_type=jnp.float32)
            cross[:, d * tok : (d + 1) * tok] = product[:tok, :tok] + (product[:tok, tok:] + product[tok:, :tok])
        if used < steps:
            cross[:, used * tok :] = jnp.zeros_like(cross[:, used * tok :])
        skewed = pltpu.roll(cross[...], width - tok + 1, 1, stride=1, stride_axis=0)
        lag_sums[pl.ds(g, 1), :] = jnp.sum(skewed, axis=0, keepdims=True)[:, : width - tok] * scale

    for a in range(blocks):
        if out_ref.shape[2] > groups * per:
            out_ref[a, :tok, :] = jnp.zeros_like(out_ref[a, :tok, :])
        out_ref[a, :tok, : groups * per] = grads[:, a * per : (a + 1) * per, :].reshape(groups * per, tok).T
        out_ref[a, tok:, :] = jnp.zeros_like(out_ref[a, tok:, :])
        out_ref[a, tok : tok + groups, :lag_own] = lag_sums[:, a * lag_own : (a + 1) * lag_own]


def convolve(seq_blocks, input_blocks, moved, lag_own, scale):
    blocks, tok, own = seq_blocks.shape
    groups, _, width = moved.shape
    channels = own // groups
    per = -(-channels // ROW_TILE) * ROW_TILE
    if groups * per != LANES or channels != per:
        wide = groups * per
        lanes = -(-wide // LANES) * LANES

        def widen(v):
            v = v.reshape(blocks, tok, groups, channels)
            v = jnp.pad(v, ((0, 0), (0, 0), (0, 0), (0, per - channels))).reshape(blocks, tok, wide)
            return jnp.pad(v, ((0, 0), (0, 0), (0, lanes - wide)))

        seq_blocks, input_blocks = widen(seq_blocks), widen(input_blocks)
    rows = blocks * per
    steps = min(width // tok, blocks)
    extra = -(-groups // 8) * 8
    out_lanes = max(groups * per, lag_own)
    out = pl.pallas_call(
        functools.partial(conv_kernel, scale, lag_own),
        in_specs=[VMEM] * 3,
        out_specs=VMEM,
        out_shape=jax.ShapeDtypeStruct((blocks, tok + extra, out_lanes), jnp.float32),
        scratch_shapes=[pltpu.VMEM((groups, 2 * rows, tok), jnp.bfloat16)] * 2
        + [pltpu.VMEM((groups, rows, tok), jnp.bfloat16)] * 2
        + [
            pltpu.VMEM((rows, tok), jnp.float32),
            pltpu.VMEM((groups, rows, tok), jnp.float32),
            pltpu.VMEM((tok, width), jnp.float32),
            pltpu.VMEM((groups, width - tok), jnp.float32),
        ],
        compiler_params=pltpu.CompilerParams(vmem_limit_bytes=48 * 1024 * 1024),
        cost_estimate=pl.CostEstimate(
            flops=groups * rows * tok * tok * steps * 16,
            bytes_accessed=12 * blocks * tok * LANES + 4 * groups * tok * width,
            transcendentals=0,
        ),
        name="convolve",
    )(seq_blocks, input_blocks, moved)
    return out


def ring_chip(place, chips):
    place = lax.rem(place + chips, chips)
    return jnp.where(place < chips // 2, 2 * place, 2 * (chips - 1 - place) + 1)


def ring_pairs(chips, forward):
    order = list(range(0, chips, 2)) + list(range(chips - 1, 0, -2))
    pairs = [(2 * order[p] + k, 2 * order[(p + 1) % chips] + k) for p in range(chips) for k in range(2)]
    return pairs if forward else [(b, a) for a, b in pairs]


def pair_cotangent(cotangent, features):
    tok, held = cotangent.shape
    parts = lax.axis_size("ch")
    core = lax.rem(lax.axis_index("ctx"), 2)
    swap = [(i, i ^ 1) for i in range(lax.axis_size("ctx"))]
    pieces = [cotangent]
    for s in range(1, parts):
        pieces.append(lax.ppermute(cotangent, "ch", [(j, (j + s) % parts) for j in range(parts)]))
    mine, theirs = [], []
    for piece in pieces:
        blocks = piece.reshape(tok, held // (2 * features), 2, features)
        mine.append(lax.dynamic_index_in_dim(blocks, core, 2, keepdims=False).reshape(tok, held // 2))
        theirs.append(lax.dynamic_index_in_dim(blocks, 1 - core, 2, keepdims=False).reshape(tok, held // 2))
    arrived = lax.ppermute(jnp.concatenate(theirs, axis=1), "ctx", swap)
    return jnp.concatenate([jnp.concatenate(mine, axis=1), arrived], axis=0)


def project(cotangent, out_weight, chains):
    tok = cotangent.shape[0]
    channels, features = out_weight.shape
    devices = lax.axis_size("ctx")
    chips = devices // 2
    parts = lax.axis_size("ch")
    chip = lax.axis_index("ctx") // 2
    place = jnp.where(chip % 2 == 0, chip // 2, chips - 1 - chip // 2)
    both = pair_cotangent(cotangent, features)
    rows = channels // chains
    held = [out_weight[c * rows : (c + 1) * rows] for c in range(chains)]
    sums = [None] * chains
    chips_of_part = chips // parts
    for step in range(chips):
        for c in range(chains):
            source = ring_chip(place - step if c % 2 == 0 else place + step, chips)
            slot = lax.rem(lax.axis_index("ch") - source // chips_of_part + parts, parts)
            column = (slot * chips_of_part + lax.rem(source, chips_of_part)) * features
            term = lax.dot_general(
                lax.dynamic_slice_in_dim(both, column, features, 1),
                held[c],
                (((1,), (1,)), ((), ())),
                preferred_element_type=jnp.float32,
            )
            sums[c] = term if step == 0 else sums[c] + term
        if step < chips - 1:
            held = [lax.ppermute(v, "ctx", ring_pairs(chips, c % 2 == 0)) for c, v in enumerate(held)]
    swap = [(i, i ^ 1) for i in range(devices)]
    done = [v[:tok] + lax.ppermute(v[tok:], "ctx", swap) for v in sums]
    return jnp.concatenate(done, axis=1)


def body(cotangent, out_weight, gate_value, conv_output, conv_input, filters):
    tok, channels = gate_value.shape
    all_groups, lags = filters.shape
    devices = lax.axis_size("ctx")
    per_group = channels // all_groups
    own = channels // devices
    groups = max(1, own // per_group)
    share = max(1, per_group // own)
    lag_own = lags // devices
    me = lax.axis_index("ctx")

    def to_channels(v):
        blocks = v.reshape(tok, devices, own).transpose(1, 0, 2)
        return lax.all_to_all(blocks, "ctx", 0, 0, tiled=True)

    input_blocks = to_channels(conv_input[::-1])
    own_filters = lax.dynamic_slice_in_dim(filters, me * own // per_group, groups, 0)
    moved = toeplitz(own_filters, tok)

    grad_out = project(cotangent, out_weight, 2)
    gate_grad = grad_out * conv_output
    seq_blocks = to_channels(grad_out * gate_value)

    scale = 1.0 / math.sqrt(per_group * tok * devices)
    result = convolve(seq_blocks, input_blocks, moved, lag_own, scale)
    back = lax.all_to_all(result[:, :, : max(own, lag_own)], "ctx", 0, 0, tiled=True)
    input_grad = back[:, :tok, :own].transpose(1, 0, 2).reshape(tok, channels)
    filter_grad = back[:, tok : tok + groups, :lag_own].reshape(all_groups, share, lag_own).sum(axis=1)
    return (input_grad, gate_grad, filter_grad)


def solution(mesh):
    return jax.shard_map(
        body,
        mesh=mesh,
        in_specs=(
            P("ctx", "ch"),
            P("ch", "ctx"),
            P("ctx", "ch"),
            P("ctx", "ch"),
            P("ctx", "ch"),
            P("ch", None),
        ),
        out_specs=(P("ctx", "ch"), P("ctx", "ch"), P("ch", "ctx")),
        check_vma=False,
    )
```

```python
import functools
import math

import jax
import jax.numpy as jnp
from jax import lax
from jax.experimental import pallas as pl
from jax.experimental.pallas import tpu as pltpu
from jax.sharding import PartitionSpec as P

LANES = 128
ROW_TILE = 16
CODE_UNIT = 8192.0
SMALLEST = 1e-30
VMEM = pl.BlockSpec(memory_space=pltpu.VMEM)


def split(value):
    high = value.astype(jnp.bfloat16)
    return high, (value - high.astype(jnp.float32)).astype(jnp.bfloat16)


def toeplitz_kernel(filter_ref, out_ref):
    tok = out_ref.shape[1] // 2
    rows = jnp.broadcast_to(filter_ref[0], (tok, filter_ref.shape[2]))
    high, low = split(pltpu.roll(rows, 0, 1, stride=1, stride_axis=0))
    out_ref[0, :tok, :] = high
    out_ref[0, tok:, :] = low


def toeplitz(filters, tok):
    groups, lags = filters.shape
    width = lags + tok
    padded = jnp.pad(filters, ((0, 0), (0, tok)))[:, None, :]
    return pl.pallas_call(
        toeplitz_kernel,
        grid=(groups,),
        in_specs=[pl.BlockSpec((1, 1, width), lambda g: (g, 0, 0))],
        out_specs=pl.BlockSpec((1, 2 * tok, width), lambda g: (g, 0, 0)),
        out_shape=jax.ShapeDtypeStruct((groups, 2 * tok, width), jnp.bfloat16),
        cost_estimate=pl.CostEstimate(
            flops=groups * tok * width * 4, bytes_accessed=groups * width * (4 + 4 * tok), transcendentals=0
        ),
        name="toeplitz",
    )(padded)


def stack_kernel(x_ref, left_ref, x_hi, x_lo):
    blocks, tok, _ = x_ref.shape
    groups, rows, _ = x_hi.shape
    per = rows // blocks

    @pl.loop(0, blocks)
    def _(a):
        at = pl.ds(pl.multiple_of(a * per, per), per)
        high, low = split(x_ref[a].T[: groups * per])
        x_hi[:, at, :] = high.reshape(groups, per, tok)
        x_lo[:, at, :] = low.reshape(groups, per, tok)

    @pl.loop(0, groups)
    def _(g):
        left_ref[g] = jnp.concatenate([x_hi[g], x_lo[g]], axis=1).T


def stack_input(input_blocks, groups, per):
    blocks, tok, lanes = input_blocks.shape
    rows = blocks * per
    return pl.pallas_call(
        stack_kernel,
        in_specs=[VMEM],
        out_specs=VMEM,
        out_shape=jax.ShapeDtypeStruct((groups, 2 * tok, rows), jnp.bfloat16),
        scratch_shapes=[pltpu.VMEM((groups, rows, tok), jnp.bfloat16)] * 2,
        compiler_params=pltpu.CompilerParams(vmem_limit_bytes=32 * 1024 * 1024),
        cost_estimate=pl.CostEstimate(
            flops=blocks * tok * lanes * 8, bytes_accessed=blocks * tok * lanes * 8, transcendentals=0
        ),
        name="stack_input",
    )(input_blocks)


def coded(value, most):
    exponent = jnp.floor(jnp.log2(jnp.maximum(most, SMALLEST)))
    v = value * jnp.exp2(-exponent)
    return v * jnp.abs(v) * CODE_UNIT, exponent


def decoded(code, exponent):
    code = code.astype(jnp.float32)
    return jnp.sign(code) * jnp.sqrt(jnp.abs(code) * (1.0 / CODE_UNIT)) * jnp.exp2(exponent.astype(jnp.float32))


def largest(value):
    return jnp.max(jnp.max(jnp.abs(value), axis=0, keepdims=True), axis=1, keepdims=True)


def conv_kernel(scale, lag_own, s_ref, left_ref, t_ref, out_ref, s_hi, s_lo, grads, cross, lag_sums):
    blocks, tok, _ = s_ref.shape
    groups, rows, _ = grads.shape
    per = rows // blocks
    width = t_ref.shape[2]
    steps = width // tok
    used = min(steps, blocks)
    g = pl.program_id(0)

    @pl.when(g == 0)
    def _():
        s_hi[:, rows:, :] = jnp.zeros_like(s_hi[:, rows:, :])
        s_lo[:, rows:, :] = jnp.zeros_like(s_lo[:, rows:, :])
        for a in range(blocks):
            high, low = split(s_ref[a].T[: groups * per])
            s_hi[:, a * per : (a + 1) * per, :] = high.reshape(groups, per, tok)
            s_lo[:, a * per : (a + 1) * per, :] = low.reshape(groups, per, tok)

    for d in range(0, used, 2):
        first, second = d * per, (d + 1) * per
        count = rows - first
        left = jnp.concatenate(
            [
                jnp.concatenate([ref[g, first : first + count, :], ref[g, second : second + count, :]], axis=1)
                for ref in (s_hi, s_lo)
            ],
            axis=0,
        )
        if d + 2 <= steps:
            right = t_ref[0, :, d * tok : (d + 2) * tok]
        else:
            right = jnp.concatenate([t_ref[0, :, d * tok :], jnp.zeros((2 * tok, tok), jnp.bfloat16)], axis=1)
        product = lax.dot_general(left, right, (((1,), (1,)), ((), ())), preferred_element_type=jnp.float32)
        term = product[:count, :tok] + (product[:count, tok:] + product[count:, :tok])
        if d == 0:
            grads[g] = term
        else:
            grads[g, :count, :] += term

    for d in range(0, used, 2):
        depth = min(rows, -(-(rows - d * per) // LANES) * LANES)
        high, low = [
            jnp.concatenate([ref[g, d * per : d * per + depth, :], ref[g, (d + 1) * per : (d + 1) * per + depth, :]], axis=1)
            for ref in (s_hi, s_lo)
        ]
        main = jnp.dot(left_ref[0, :, :depth], high, preferred_element_type=jnp.float32)
        rest = jnp.dot(left_ref[0, :tok, :depth], low, preferred_element_type=jnp.float32)
        stop = min(d + 2, steps)
        cross[:, d * tok : stop * tok] = (main[:tok] + (main[tok:] + rest))[:, : (stop - d) * tok]
    if used + used % 2 < steps:
        cross[:, (used + used % 2) * tok :] = jnp.zeros_like(cross[:, (used + used % 2) * tok :])
    skewed = pltpu.roll(cross[...], width - tok + 1, 1, stride=1, stride_axis=0)
    lag_sums[pl.ds(g, 1), :] = jnp.sum(skewed, axis=0, keepdims=True)[:, : width - tok] * scale

    @pl.when(g == groups - 1)
    def _():
        lags, lag_exponent = coded(lag_sums[...], largest(lag_sums[...]))
        held = out_ref.shape[1] - 8
        for a in range(blocks):
            out_ref[a, tok:held, :] = jnp.zeros_like(out_ref[a, tok:held, :])
            block = grads[:, a * per : (a + 1) * per, :].reshape(groups * per, tok)
            code, exponent = coded(block, largest(block))
            if out_ref.shape[2] > groups * per:
                out_ref[a, :tok, :] = jnp.zeros_like(out_ref[a, :tok, :])
            out_ref[a, :tok, : groups * per] = code.T
            out_ref[a, tok : tok + groups, :lag_own] = lags[:, a * lag_own : (a + 1) * lag_own]
            which = lax.broadcasted_iota(jnp.int32, (8, out_ref.shape[2]), 0)
            out_ref[a, held:, :] = jnp.where(which == 0, exponent, lag_exponent)


def convolve(seq_blocks, input_blocks, moved, channels, lag_own, scale):
    blocks, tok, own = seq_blocks.shape
    groups, _, width = moved.shape
    per = -(-channels // ROW_TILE) * ROW_TILE
    if groups * per != LANES or channels != per:
        wide = groups * per
        lanes = -(-wide // LANES) * LANES

        def widen(v):
            v = v.reshape(blocks, tok, groups, channels)
            v = jnp.pad(v, ((0, 0), (0, 0), (0, 0), (0, per - channels))).reshape(blocks, tok, wide)
            return jnp.pad(v, ((0, 0), (0, 0), (0, lanes - wide)))

        seq_blocks, input_blocks = widen(seq_blocks), widen(input_blocks)
    rows = blocks * per
    left = stack_input(input_blocks, groups, per)
    extra = -(-(groups + 8) // ROW_TILE) * ROW_TILE
    out_lanes = max(groups * per, lag_own)
    return pl.pallas_call(
        functools.partial(conv_kernel, scale, lag_own),
        grid=(groups,),
        in_specs=[
            pl.BlockSpec(seq_blocks.shape, lambda g: (0, 0, 0)),
            pl.BlockSpec((1, 2 * tok, rows), lambda g: (g, 0, 0)),
            pl.BlockSpec((1, 2 * tok, width), lambda g: (g, 0, 0)),
        ],
        out_specs=pl.BlockSpec((blocks, tok + extra, out_lanes), lambda g: (0, 0, 0)),
        out_shape=jax.ShapeDtypeStruct((blocks, tok + extra, out_lanes), jnp.float32),
        scratch_shapes=[pltpu.VMEM((groups, 2 * rows, tok), jnp.bfloat16)] * 2
        + [
            pltpu.VMEM((groups, rows, tok), jnp.float32),
            pltpu.VMEM((tok, width), jnp.float32),
            pltpu.VMEM((groups, width - tok), jnp.float32),
        ],
        compiler_params=pltpu.CompilerParams(vmem_limit_bytes=48 * 1024 * 1024),
        cost_estimate=pl.CostEstimate(
            flops=groups * rows * tok * width * 14,
            bytes_accessed=12 * blocks * tok * LANES + 4 * groups * tok * width,
            transcendentals=0,
        ),
        name="convolve",
    )(seq_blocks, left, moved)


def ring_chip(place, chips):
    place = lax.rem(place + chips, chips)
    return jnp.where(place < chips // 2, 2 * place, 2 * (chips - 1 - place) + 1)


def ring_pairs(chips, forward):
    order = list(range(0, chips, 2)) + list(range(chips - 1, 0, -2))
    pairs = [(2 * order[p] + k, 2 * order[(p + 1) % chips] + k) for p in range(chips) for k in range(2)]
    return pairs if forward else [(b, a) for a, b in pairs]


def pair_cotangent(cotangent, features):
    tok, held = cotangent.shape
    parts = lax.axis_size("ch")
    core = lax.rem(lax.axis_index("ctx"), 2)
    swap = [(i, i ^ 1) for i in range(lax.axis_size("ctx"))]
    pieces = [cotangent]
    for s in range(1, parts):
        pieces.append(lax.ppermute(cotangent, "ch", [(j, (j + s) % parts) for j in range(parts)]))
    mine, theirs = [], []
    for piece in pieces:
        blocks = piece.reshape(tok, held // (2 * features), 2, features)
        mine.append(lax.dynamic_index_in_dim(blocks, core, 2, keepdims=False).reshape(tok, held // 2))
        theirs.append(lax.dynamic_index_in_dim(blocks, 1 - core, 2, keepdims=False).reshape(tok, held // 2))
    arrived = lax.ppermute(jnp.concatenate(theirs, axis=1), "ctx", swap)
    return jnp.concatenate([jnp.concatenate(mine, axis=1), arrived], axis=0)


def seq_kernel(*refs):
    *parts, gate_ref, out_ref = refs
    count = len(parts) // 2
    blocks, tok, own = out_ref.shape
    width = parts[0].shape[1]
    for b in range(blocks):
        c, at = divmod(b * own, width)
        grad_out = parts[c][:, at : at + own] + parts[count + c][:, at : at + own]
        out_ref[b] = grad_out * gate_ref[:, b * own : (b + 1) * own]


def seq_blocks_of(sums, arrived, gate_value, blocks):
    tok, channels = gate_value.shape
    return pl.pallas_call(
        seq_kernel,
        in_specs=[VMEM] * (2 * len(sums) + 1),
        out_specs=VMEM,
        out_shape=jax.ShapeDtypeStruct((blocks, tok, channels // blocks), jnp.float32),
        compiler_params=pltpu.CompilerParams(vmem_limit_bytes=32 * 1024 * 1024),
        cost_estimate=pl.CostEstimate(
            flops=2 * tok * channels, bytes_accessed=16 * tok * channels, transcendentals=0
        ),
        name="seq_grad",
    )(*sums, *arrived, gate_value)


def project(cotangent, out_weight, chains):
    tok = cotangent.shape[0]
    channels, features = out_weight.shape
    devices = lax.axis_size("ctx")
    chips = devices // 2
    parts = lax.axis_size("ch")
    chip = lax.axis_index("ctx") // 2
    place = jnp.where(chip % 2 == 0, chip // 2, chips - 1 - chip // 2)
    both = pair_cotangent(cotangent, features)
    rows = channels // chains
    held = [out_weight[c * rows : (c + 1) * rows] for c in range(chains)]
    sums = [[None, None] for _ in range(chains)]
    chips_of_part = chips // parts
    for step in range(chips):
        for c in range(chains):
            source = ring_chip(place - step if c % 2 == 0 else place + step, chips)
            slot = lax.rem(lax.axis_index("ch") - source // chips_of_part + parts, parts)
            column = (slot * chips_of_part + lax.rem(source, chips_of_part)) * features
            for half in (1, 0):
                term = lax.dot_general(
                    lax.dynamic_slice(both, (half * tok, column), (tok, features)),
                    held[c],
                    (((1,), (1,)), ((), ())),
                    preferred_element_type=jnp.float32,
                )
                sums[c][half] = term if step == 0 else sums[c][half] + term
        if step < chips - 1:
            held = [lax.ppermute(v, "ctx", ring_pairs(chips, c % 2 == 0)) for c, v in enumerate(held)]
    swap = [(i, i ^ 1) for i in range(devices)]
    return [own for own, _ in sums], [lax.ppermute(other, "ctx", swap) for _, other in sums]


def body(cotangent, out_weight, gate_value, conv_output, conv_input, filters):
    tok, channels = gate_value.shape
    all_groups, lags = filters.shape
    devices = lax.axis_size("ctx")
    per_group = channels // all_groups
    own = channels // devices
    groups = max(1, own // per_group)
    share = max(1, per_group // own)
    lag_own = lags // devices
    me = lax.axis_index("ctx")

    def exchange(blocks):
        return lax.all_to_all(blocks, "ctx", 0, 0, tiled=True)

    code, exponent = coded(conv_input[::-1], largest(conv_input))
    code = code.reshape(tok, devices, own).transpose(1, 0, 2)
    code = jnp.concatenate([code, jnp.broadcast_to(exponent, (devices, ROW_TILE, own))], axis=1)
    code = exchange(code.astype(jnp.float16))
    input_blocks = decoded(code[:, :tok], code[:, tok : tok + 1, :1])
    own_filters = lax.dynamic_slice_in_dim(filters, me * own // per_group, groups, 0)
    moved = toeplitz(own_filters, tok)

    sums, arrived = project(cotangent, out_weight, 2)
    seq_blocks = exchange(seq_blocks_of(sums, arrived, gate_value, devices))
    grad_out = jnp.concatenate([a + b for a, b in zip(sums, arrived)], axis=1)
    gate_grad = grad_out * conv_output

    scale = 1.0 / math.sqrt(per_group * tok * devices)
    result = convolve(seq_blocks, input_blocks, moved, min(own, per_group), lag_own, scale)
    back = exchange(result[:, :, : max(own, lag_own)].astype(jnp.float16))
    held = back.shape[1] - 8
    input_grad = decoded(back[:, :tok, :own], back[:, held : held + 1, :1])
    input_grad = input_grad.transpose(1, 0, 2).reshape(tok, channels)
    filter_grad = decoded(back[:, tok : tok + groups, :lag_own], back[:, held + 1 : held + 2, :1])
    filter_grad = filter_grad.reshape(all_groups, share, lag_own).sum(axis=1)
    return (input_grad, gate_grad, filter_grad)


def solution(mesh):
    return jax.shard_map(
        body,
        mesh=mesh,
        in_specs=(
            P("ctx", "ch"),
            P("ch", "ctx"),
            P("ctx", "ch"),
            P("ctx", "ch"),
            P("ctx", "ch"),
            P("ch", None),
        ),
        out_specs=(P("ctx", "ch"), P("ctx", "ch"), P("ch", "ctx")),
        check_vma=False,
    )
```

```python
import functools
import math

import jax
import jax.numpy as jnp
from jax import lax
from jax.experimental import pallas as pl
from jax.experimental.pallas import tpu as pltpu
from jax.sharding import PartitionSpec as P

LANES = 128
ROW_TILE = 16
GRANT = 60 * 1024 * 1024
CODE_UNIT = 8192.0
SMALLEST = 1e-30
VMEM = pl.BlockSpec(memory_space=pltpu.VMEM)
SMEM = pl.BlockSpec(memory_space=pltpu.SMEM)
ANY = pl.BlockSpec(memory_space=pl.ANY)


def split(value):
    high = value.astype(jnp.bfloat16)
    return high, (value - high.astype(jnp.float32)).astype(jnp.bfloat16)


def toeplitz_kernel(filter_ref, out_ref):
    tok = out_ref.shape[1] // 2
    rows = jnp.broadcast_to(filter_ref[0], (tok, filter_ref.shape[2]))
    high, low = split(pltpu.roll(rows, 0, 1, stride=1, stride_axis=0))
    out_ref[0, :tok, :] = high
    out_ref[0, tok:, :] = low


def toeplitz(filters, tok):
    groups, lags = filters.shape
    width = lags + tok
    padded = jnp.pad(filters, ((0, 0), (0, tok)))[:, None, :]
    return pl.pallas_call(
        toeplitz_kernel,
        grid=(groups,),
        in_specs=[pl.BlockSpec((1, 1, width), lambda g: (g, 0, 0))],
        out_specs=pl.BlockSpec((1, 2 * tok, width), lambda g: (g, 0, 0)),
        out_shape=jax.ShapeDtypeStruct((groups, 2 * tok, width), jnp.bfloat16),
        cost_estimate=pl.CostEstimate(
            flops=groups * tok * width * 4, bytes_accessed=groups * width * (4 + 4 * tok), transcendentals=0
        ),
        name="toeplitz",
    )(padded)


def stack_kernel(x_ref, left_ref, x_hi, x_lo):
    blocks, tok, _ = x_ref.shape
    groups, rows, _ = x_hi.shape
    per = rows // blocks

    @pl.loop(0, blocks)
    def _(a):
        at = pl.ds(pl.multiple_of(a * per, per), per)
        high, low = split(x_ref[a].T[: groups * per])
        x_hi[:, at, :] = high.reshape(groups, per, tok)
        x_lo[:, at, :] = low.reshape(groups, per, tok)

    last = lax.broadcasted_iota(jnp.int32, (tok, tok), 0) + lax.broadcasted_iota(jnp.int32, (tok, tok), 1)
    turn = jnp.where(last == tok - 1, 1.0, 0.0).astype(jnp.bfloat16)

    @pl.loop(0, groups)
    def _(g):
        for half, ref in ((0, x_hi), (1, x_lo)):
            turned = lax.dot_general(turn, ref[g], (((1,), (1,)), ((), ())), preferred_element_type=jnp.float32)
            left_ref[g, half * tok : (half + 1) * tok, :] = turned.astype(jnp.bfloat16)


def stack_input(input_blocks, groups, per):
    blocks, tok, lanes = input_blocks.shape
    rows = blocks * per
    return pl.pallas_call(
        stack_kernel,
        in_specs=[VMEM],
        out_specs=VMEM,
        out_shape=jax.ShapeDtypeStruct((groups, 2 * tok, rows), jnp.bfloat16),
        scratch_shapes=[pltpu.VMEM((groups, rows, tok), jnp.bfloat16)] * 2,
        compiler_params=pltpu.CompilerParams(vmem_limit_bytes=32 * 1024 * 1024),
        cost_estimate=pl.CostEstimate(
            flops=blocks * tok * lanes * 8, bytes_accessed=blocks * tok * lanes * 8, transcendentals=0
        ),
        name="stack_input",
    )(input_blocks)


def coded(value, most):
    exponent = jnp.floor(jnp.log2(jnp.maximum(most, SMALLEST)))
    v = value * jnp.exp2(-exponent)
    return v * jnp.abs(v) * CODE_UNIT, exponent


def decoded(code, exponent):
    code = code.astype(jnp.float32)
    return jnp.sign(code) * jnp.sqrt(jnp.abs(code) * (1.0 / CODE_UNIT)) * jnp.exp2(exponent.astype(jnp.float32))


def largest(value):
    return jnp.max(jnp.max(jnp.abs(value), axis=0, keepdims=True), axis=1, keepdims=True)


def conv_kernel(scale, lag_own, s_ref, left_ref, t_ref, out_ref, s_hi, s_lo, grads, cross, lag_sums):
    blocks, tok = 2 * s_ref.shape[0] * s_ref.shape[1], s_ref.shape[3]
    groups, rows, _ = grads.shape
    per = rows // blocks
    width = t_ref.shape[2]
    steps = width // tok
    used = min(steps, blocks)
    g = pl.program_id(0)

    @pl.when(g == 0)
    def _():
        s_hi[:, rows:, :] = jnp.zeros_like(s_hi[:, rows:, :])
        s_lo[:, rows:, :] = jnp.zeros_like(s_lo[:, rows:, :])
        for a in range(blocks):
            z, rest = divmod(a, s_ref.shape[1])
            high, low = split(s_ref[z // 2, rest, z % 2].T[: groups * per])
            s_hi[:, a * per : (a + 1) * per, :] = high.reshape(groups, per, tok)
            s_lo[:, a * per : (a + 1) * per, :] = low.reshape(groups, per, tok)

    for d in range(0, used, 2):
        first, second = d * per, (d + 1) * per
        count = rows - first
        left = jnp.concatenate(
            [
                jnp.concatenate([ref[g, first : first + count, :], ref[g, second : second + count, :]], axis=1)
                for ref in (s_hi, s_lo)
            ],
            axis=0,
        )
        if d + 2 <= steps:
            right = t_ref[0, :, d * tok : (d + 2) * tok]
        else:
            right = jnp.concatenate([t_ref[0, :, d * tok :], jnp.zeros((2 * tok, tok), jnp.bfloat16)], axis=1)
        product = lax.dot_general(left, right, (((1,), (1,)), ((), ())), preferred_element_type=jnp.float32)
        term = product[:count, :tok] + (product[:count, tok:] + product[count:, :tok])
        if d == 0:
            grads[g] = term
        else:
            grads[g, :count, :] += term

    for d in range(0, used, 2):
        depth = min(rows, -(-(rows - d * per) // LANES) * LANES)
        high, low = [
            jnp.concatenate([ref[g, d * per : d * per + depth, :], ref[g, (d + 1) * per : (d + 1) * per + depth, :]], axis=1)
            for ref in (s_hi, s_lo)
        ]
        main = jnp.dot(left_ref[0, :, :depth], high, preferred_element_type=jnp.float32)
        rest = jnp.dot(left_ref[0, :tok, :depth], low, preferred_element_type=jnp.float32)
        stop = min(d + 2, steps)
        cross[:, d * tok : stop * tok] = (main[:tok] + (main[tok:] + rest))[:, : (stop - d) * tok]
    if used + used % 2 < steps:
        cross[:, (used + used % 2) * tok :] = jnp.zeros_like(cross[:, (used + used % 2) * tok :])
    skewed = pltpu.roll(cross[...], width - tok + 1, 1, stride=1, stride_axis=0)
    lag_sums[pl.ds(g, 1), :] = jnp.sum(skewed, axis=0, keepdims=True)[:, : width - tok] * scale

    @pl.when(g == groups - 1)
    def _():
        lags, lag_exponent = coded(lag_sums[...], largest(lag_sums[...]))
        held = out_ref.shape[1] - 8
        for a in range(blocks):
            out_ref[a, tok:held, :] = jnp.zeros_like(out_ref[a, tok:held, :])
            block = grads[:, a * per : (a + 1) * per, :].reshape(groups * per, tok)
            code, exponent = coded(block, largest(block))
            if out_ref.shape[2] > groups * per:
                out_ref[a, :tok, :] = jnp.zeros_like(out_ref[a, :tok, :])
            out_ref[a, :tok, : groups * per] = code.T
            out_ref[a, tok : tok + groups, :lag_own] = lags[:, a * lag_own : (a + 1) * lag_own]
            which = lax.broadcasted_iota(jnp.int32, (8, out_ref.shape[2]), 0)
            out_ref[a, held:, :] = jnp.where(which == 0, exponent, lag_exponent)


def convolve(seq_blocks, input_blocks, moved, channels, lag_own, scale):
    blocks, tok, own = input_blocks.shape
    groups, _, width = moved.shape
    per = -(-channels // ROW_TILE) * ROW_TILE
    if groups * per != LANES or channels != per:
        wide = groups * per
        lanes = -(-wide // LANES) * LANES

        def widen(v):
            shape = v.shape[:-1]
            v = v.reshape(-1, groups, channels)
            v = jnp.pad(v, ((0, 0), (0, 0), (0, per - channels))).reshape(-1, wide)
            return jnp.pad(v, ((0, 0), (0, lanes - wide))).reshape(shape + (lanes,))

        seq_blocks, input_blocks = widen(seq_blocks), widen(input_blocks)
    rows = blocks * per
    left = stack_input(input_blocks, groups, per)
    extra = -(-(groups + 8) // ROW_TILE) * ROW_TILE
    out_lanes = max(groups * per, lag_own)
    return pl.pallas_call(
        functools.partial(conv_kernel, scale, lag_own),
        grid=(groups,),
        in_specs=[
            pl.BlockSpec(seq_blocks.shape, lambda g: (0, 0, 0, 0, 0)),
            pl.BlockSpec((1, 2 * tok, rows), lambda g: (g, 0, 0)),
            pl.BlockSpec((1, 2 * tok, width), lambda g: (g, 0, 0)),
        ],
        out_specs=pl.BlockSpec((blocks, tok + extra, out_lanes), lambda g: (0, 0, 0)),
        out_shape=jax.ShapeDtypeStruct((blocks, tok + extra, out_lanes), jnp.float32),
        scratch_shapes=[pltpu.VMEM((groups, 2 * rows, tok), jnp.bfloat16)] * 2
        + [
            pltpu.VMEM((groups, rows, tok), jnp.float32),
            pltpu.VMEM((tok, width), jnp.float32),
            pltpu.VMEM((groups, width - tok), jnp.float32),
        ],
        compiler_params=pltpu.CompilerParams(vmem_limit_bytes=48 * 1024 * 1024),
        cost_estimate=pl.CostEstimate(
            flops=groups * rows * tok * width * 14,
            bytes_accessed=12 * blocks * tok * LANES + 4 * groups * tok * width,
            transcendentals=0,
        ),
        name="convolve",
    )(seq_blocks, left, moved)


def nothing(*refs):
    del refs


def after(value, *earlier):
    return pl.pallas_call(
        nothing,
        in_specs=[ANY] * (1 + len(earlier)),
        out_specs=ANY,
        out_shape=jax.ShapeDtypeStruct(value.shape, value.dtype),
        input_output_aliases={0: 0},
        cost_estimate=pl.CostEstimate(flops=0, bytes_accessed=0, transcendentals=0),
        name="after",
    )(value, *earlier)


class Place:
    def __init__(self):
        self.devices = lax.axis_size("ctx")
        self.ys = self.devices // 8
        assert self.devices == 8 * self.ys
        me = lax.axis_index("ctx")
        self.core, chip = lax.rem(me, 2), me // 2
        self.y, z = lax.rem(chip, self.ys), chip // self.ys
        self.p, self.h = lax.rem(z, 2), z // 2
        self.block = (self.h * self.ys + self.y) * 2 + self.core

    def index(self, h, p, y, core):
        return ((h * 2 + p) * self.ys + y) * 2 + core

    def all(self):
        return [(h, p, y, c) for h in range(2) for p in range(2) for y in range(self.ys) for c in range(2)]

    def swap_core(self, v):
        return lax.ppermute(v, "ctx", [(self.index(h, p, y, c), self.index(h, p, y, 1 - c)) for h, p, y, c in self.all()])

    def swap_pair(self, v):
        return lax.ppermute(v, "ctx", [(self.index(h, p, y, c), self.index(h, 1 - p, y, c)) for h, p, y, c in self.all()])

    def swap_half(self, v):
        return lax.ppermute(v, "ctx", [(self.index(h, p, y, c), self.index(1 - h, p, y, c)) for h, p, y, c in self.all()])

    def swap_half_and_pair(self, v):
        pairs = [(self.index(h, p, y, c), self.index(1 - h, 1 - p, y, c)) for h, p, y, c in self.all()]
        return lax.ppermute(v, "ctx", pairs)

    def along_y(self, v, shift):
        ys = self.ys
        return lax.ppermute(
            v, "ctx", [(self.index(h, p, y, c), self.index(h, p, (y + shift) % ys, c)) for h, p, y, c in self.all()]
        )

    def same_p(self):
        return [[self.index(h, p, y, c) for h in range(2) for y in range(self.ys) for c in range(2)] for p in range(2)]


def pick_kernel(features, slots, core_ref, *refs):
    parts, (mine_ref, theirs_ref) = refs[: 2 * slots], refs[-2:]
    tok, held = parts[0].shape
    first = core_ref[0] == 0
    for row in range(2):
        rows = slice(row * tok, (row + 1) * tok)
        for s in range(slots):
            part = parts[row * slots + s]
            for b in range(held // (2 * features)):
                even = part[:, 2 * b * features : (2 * b + 1) * features]
                odd = part[:, (2 * b + 1) * features : (2 * b + 2) * features]
                at = s * held // 2 + b * features
                mine_ref[rows, at : at + features] = jnp.where(first, even, odd)
                theirs_ref[rows, at : at + features] = jnp.where(first, odd, even)


def gather_cotangent(cotangent, features, place, earlier):
    tok, held = cotangent.shape
    parts = lax.axis_size("ch")
    far = place.swap_pair(cotangent)

    def along_ch(v):
        return [v] + [lax.ppermute(v, "ch", [(j, (j + s) % parts) for j in range(parts)]) for s in range(1, parts)]

    whole = jax.ShapeDtypeStruct((2 * tok, parts * held // 2), cotangent.dtype)
    mine, theirs = pl.pallas_call(
        functools.partial(pick_kernel, features, parts),
        in_specs=[SMEM] + [VMEM] * (2 * parts),
        out_specs=[VMEM] * 2,
        out_shape=[whole, whole],
        compiler_params=pltpu.CompilerParams(vmem_limit_bytes=GRANT),
        cost_estimate=pl.CostEstimate(flops=0, bytes_accessed=8 * tok * held * parts, transcendentals=0),
        name="pick_features",
    )(place.core.reshape(1), *along_ch(cotangent), *along_ch(far))
    return mine, place.swap_core(after(theirs, *earlier))


def seq_kernel(p_ref, sum_ref, arrived_ref, gate_ref, far_gate_ref, out_ref, near_ref, far_ref):
    p = p_ref[0]
    blocks, _, tok, own = out_ref.shape
    near_ref[...] = sum_ref[:tok, :] + arrived_ref[:tok, :]
    far_ref[...] = sum_ref[tok:, :] + arrived_ref[tok:, :]
    near = near_ref[...] * gate_ref[...]
    far = far_ref[...] * far_gate_ref[...]
    for b in range(blocks):
        out_ref[b, p] = near[:, b * own : (b + 1) * own]
        out_ref[b, 1 - p] = far[:, b * own : (b + 1) * own]


def seq_blocks_of(total, arrived, gate_value, far_gate, place):
    tok, channels = gate_value.shape
    blocks = place.devices // 2
    half = channels // 2
    own = half // blocks
    steps = max(1, min(4, half // LANES))
    width, count = half // steps, blocks // steps
    return pl.pallas_call(
        seq_kernel,
        grid_spec=pltpu.PrefetchScalarGridSpec(
            num_scalar_prefetch=1,
            grid=(steps,),
            in_specs=[
                pl.BlockSpec((2 * tok, width), lambda i, p: (0, i)),
                pl.BlockSpec((2 * tok, width), lambda i, p: (0, i)),
                pl.BlockSpec((tok, width), lambda i, p: (0, p[0] * steps + i)),
                pl.BlockSpec((tok, width), lambda i, p: (0, i)),
            ],
            out_specs=[
                pl.BlockSpec((count, 2, tok, own), lambda i, p: (i, 0, 0, 0)),
                pl.BlockSpec((tok, width), lambda i, p: (0, i)),
                pl.BlockSpec((tok, width), lambda i, p: (0, i)),
            ],
        ),
        out_shape=[
            jax.ShapeDtypeStruct((blocks, 2, tok, own), jnp.float32),
            jax.ShapeDtypeStruct((tok, half), jnp.float32),
            jax.ShapeDtypeStruct((tok, half), jnp.float32),
        ],
        compiler_params=pltpu.CompilerParams(vmem_limit_bytes=GRANT),
        cost_estimate=pl.CostEstimate(
            flops=2 * tok * channels, bytes_accessed=24 * tok * channels, transcendentals=0
        ),
        name="seq_grad",
    )(place.p.reshape(1), total, arrived, gate_value, far_gate)


def share_kernel(columns_ref, mine_ref, theirs_ref, *refs):
    shares, (own_ref, other_ref) = refs[:-2], refs[-2:]
    rows, features = mine_ref.shape[0], shares[0].shape[1]
    left = []
    for s in range(len(shares)):
        at = pl.ds(pl.multiple_of(columns_ref[s], features), features)
        left.append(jnp.concatenate([mine_ref[:, at], theirs_ref[:, at]], axis=0))
    term = lax.dot_general(
        jnp.concatenate(left, axis=1),
        jnp.concatenate([share[...] for share in shares], axis=1),
        (((1,), (1,)), ((), ())),
        preferred_element_type=jnp.float32,
    )
    own_ref[...] = term[:rows]
    other_ref[...] = term[rows:]


def add_shares(columns, mine, theirs, shares):
    rows, (half, features) = mine.shape[0], shares[0].shape
    if features % LANES:
        sums = [0.0, 0.0]
        for column, share in zip(columns, shares):
            terms = [
                lax.dot_general(
                    lax.dynamic_slice_in_dim(v, column, features, 1),
                    share,
                    (((1,), (1,)), ((), ())),
                    preferred_element_type=jnp.float32,
                )
                for v in (mine, theirs)
            ]
            sums = [a + b for a, b in zip(sums, terms)]
        return sums
    tile = min(256, half)
    whole = jax.ShapeDtypeStruct((rows, half), jnp.float32)
    return pl.pallas_call(
        share_kernel,
        grid=(half // tile,),
        in_specs=[SMEM]
        + [pl.BlockSpec(mine.shape, lambda n: (0, 0))] * 2
        + [pl.BlockSpec((tile, features), lambda n: (n, 0))] * len(shares),
        out_specs=[pl.BlockSpec((rows, tile), lambda n: (0, n))] * 2,
        out_shape=[whole, whole],
        compiler_params=pltpu.CompilerParams(vmem_limit_bytes=GRANT),
        cost_estimate=pl.CostEstimate(
            flops=4 * rows * half * len(shares) * features,
            bytes_accessed=2 * (mine.size * 2 + half * len(shares) * features) + 16 * rows * half,
            transcendentals=0,
        ),
        name="add_shares",
    )(jnp.stack(columns), mine, theirs, *shares)


def project(cotangent, out_weight, place, *waited):
    channels, features = out_weight.shape
    chips = place.devices // 2
    parts = lax.axis_size("ch")
    half = channels // 2
    near = lax.dynamic_slice_in_dim(out_weight, place.p * half, half, 0)
    given = lax.dynamic_slice_in_dim(out_weight, (1 - place.p) * half, half, 0)
    far = place.swap_half(near)
    paired = place.swap_pair(given)
    far_paired = place.swap_half_and_pair(after(given, far))

    def along_y(v):
        return [v] + [place.along_y(v, shift) for shift in range(1, place.ys)]

    held = [along_y(near)]
    held.append(along_y(after(paired, *held[0][1:])))
    held.append(along_y(far))
    held.append(along_y(after(far_paired, *held[1][1:], *held[2][1:])))
    mine, theirs = gather_cotangent(cotangent, features, place, [*held[3][1:], *waited])
    chips_of_part = chips // parts

    def column(other_h, other_p, shift):
        h = 1 - place.h if other_h else place.h
        p = 1 - place.p if other_p else place.p
        source = (h * 2 + p) * place.ys + lax.rem(place.y - shift + place.ys, place.ys)
        slot = lax.rem(lax.axis_index("ch") - source // chips_of_part + parts, parts)
        return (slot * chips_of_part + lax.rem(source, chips_of_part)) * features

    shares = [
        (column(other // 2, other % 2, shift), held[other][shift]) for other in range(4) for shift in range(place.ys)
    ]
    own, other = add_shares([c for c, _ in shares], mine, theirs, [v for _, v in shares])
    return own, place.swap_core(other), far_paired


def code_kernel(x_ref, *refs):
    out_ref = refs[-1]
    devices, rows, own = out_ref.shape
    tok = x_ref.shape[0]
    code, exponent = coded(x_ref[...], largest(x_ref[...]))
    quarter = devices // 4
    for i in range(devices):
        h, p, rest = i // (2 * quarter), i // quarter % 2, i % quarter
        block = (p * 2 + h) * quarter + rest
        out_ref[i, :tok, :] = code[:, block * own : (block + 1) * own]
        out_ref[i, tok:, :] = jnp.broadcast_to(exponent, (rows - tok, own))


def code_blocks(value, devices, *awaited):
    tok, channels = value.shape
    return pl.pallas_call(
        code_kernel,
        in_specs=[VMEM] + [ANY] * len(awaited),
        out_specs=VMEM,
        out_shape=jax.ShapeDtypeStruct((devices, tok + ROW_TILE, channels // devices), jnp.float32),
        compiler_params=pltpu.CompilerParams(vmem_limit_bytes=32 * 1024 * 1024),
        cost_estimate=pl.CostEstimate(flops=4 * tok * channels, bytes_accessed=8 * tok * channels, transcendentals=0),
        name="code_input",
    )(value, *awaited)


def body(cotangent, out_weight, gate_value, conv_output, conv_input, filters):
    tok, channels = gate_value.shape
    all_groups, lags = filters.shape
    place = Place()
    devices = place.devices
    per_group = channels // all_groups
    own = channels // devices
    half = channels // 2
    groups = max(1, own // per_group)
    share = max(1, per_group // own)
    lag_own = lags // devices

    def exchange(blocks, groups=None):
        return lax.all_to_all(blocks, "ctx", 0, 0, tiled=True, axis_index_groups=groups)

    def reorder(blocks):
        return blocks.reshape((2, 2, devices // 4) + blocks.shape[1:]).swapaxes(0, 1).reshape(blocks.shape)

    far_gate = place.swap_pair(lax.dynamic_slice_in_dim(gate_value, (1 - place.p) * half, half, 1))
    total, arrived, late = project(cotangent, out_weight, place, far_gate)
    code = exchange(code_blocks(conv_input, devices, late).astype(jnp.float16))
    input_blocks = decoded(code[:, :tok], code[:, tok : tok + 1, :1])
    first_group = (place.p * half + place.block * own) // per_group
    moved = toeplitz(lax.dynamic_slice_in_dim(filters, first_group, groups, 0), tok)

    seq_blocks, near, far = seq_blocks_of(total, arrived, gate_value, far_gate, place)
    seq_blocks = exchange(seq_blocks, place.same_p())
    seq_blocks = seq_blocks.reshape(2, devices // 4, 2, tok, own)
    far = place.swap_pair(far)
    left = jnp.where(place.p == 0, near, far)
    right = jnp.where(place.p == 0, far, near)
    gate_grad = jnp.concatenate([left, right], axis=1) * conv_output

    scale = 1.0 / math.sqrt(per_group * tok * devices)
    result = convolve(seq_blocks, input_blocks, moved, min(own, per_group), lag_own, scale)
    back = exchange(result[:, :, : max(own, lag_own)].astype(jnp.float16))
    held = back.shape[1] - 8
    input_grad = reorder(decoded(back[:, :tok, :own], back[:, held : held + 1, :1]))
    input_grad = input_grad.transpose(1, 0, 2).reshape(tok, channels)
    filter_grad = reorder(decoded(back[:, tok : tok + groups, :lag_own], back[:, held + 1 : held + 2, :1]))
    filter_grad = filter_grad.reshape(all_groups, share, lag_own).sum(axis=1)
    return (input_grad, gate_grad, filter_grad)


def solution(mesh):
    return jax.shard_map(
        body,
        mesh=mesh,
        in_specs=(
            P("ctx", "ch"),
            P("ch", "ctx"),
            P("ctx", "ch"),
            P("ctx", "ch"),
            P("ctx", "ch"),
            P("ch", None),
        ),
        out_specs=(P("ctx", "ch"), P("ctx", "ch"), P("ch", "ctx")),
        check_vma=False,
    )
```

```python
import functools
import math

import jax
import jax.numpy as jnp
from jax import lax
from jax.experimental import pallas as pl
from jax.experimental.pallas import tpu as pltpu
from jax.sharding import PartitionSpec as P

LANES = 128
ROW_TILE = 16
GRANT = 60 * 1024 * 1024
CODE_UNIT = 8192.0
SMALLEST = 1e-30
VMEM = pl.BlockSpec(memory_space=pltpu.VMEM)
SMEM = pl.BlockSpec(memory_space=pltpu.SMEM)
ANY = pl.BlockSpec(memory_space=pl.ANY)


def split(value):
    high = value.astype(jnp.bfloat16)
    return high, (value - high.astype(jnp.float32)).astype(jnp.bfloat16)


def toeplitz_kernel(filter_ref, out_ref):
    tok = out_ref.shape[1] // 2
    rows = jnp.broadcast_to(filter_ref[0], (tok, filter_ref.shape[2]))
    high, low = split(pltpu.roll(rows, 0, 1, stride=1, stride_axis=0))
    out_ref[0, :tok, :] = high
    out_ref[0, tok:, :] = low


def toeplitz(filters, tok):
    groups, lags = filters.shape
    width = lags + tok
    padded = jnp.pad(filters, ((0, 0), (0, tok)))[:, None, :]
    return pl.pallas_call(
        toeplitz_kernel,
        grid=(groups,),
        in_specs=[pl.BlockSpec((1, 1, width), lambda g: (g, 0, 0))],
        out_specs=pl.BlockSpec((1, 2 * tok, width), lambda g: (g, 0, 0)),
        out_shape=jax.ShapeDtypeStruct((groups, 2 * tok, width), jnp.bfloat16),
        cost_estimate=pl.CostEstimate(
            flops=groups * tok * width * 4, bytes_accessed=groups * width * (4 + 4 * tok), transcendentals=0
        ),
        name="toeplitz",
    )(padded)


def stack_kernel(x_ref, left_ref, x_hi, x_lo):
    blocks, tok, _ = x_ref.shape
    groups, rows, _ = x_hi.shape
    per = rows // blocks

    @pl.loop(0, blocks)
    def _(a):
        at = pl.ds(pl.multiple_of(a * per, per), per)
        high, low = split(x_ref[a].T[: groups * per])
        x_hi[:, at, :] = high.reshape(groups, per, tok)
        x_lo[:, at, :] = low.reshape(groups, per, tok)

    last = lax.broadcasted_iota(jnp.int32, (tok, tok), 0) + lax.broadcasted_iota(jnp.int32, (tok, tok), 1)
    turn = jnp.where(last == tok - 1, 1.0, 0.0).astype(jnp.bfloat16)

    @pl.loop(0, groups)
    def _(g):
        for half, ref in ((0, x_hi), (1, x_lo)):
            turned = lax.dot_general(turn, ref[g], (((1,), (1,)), ((), ())), preferred_element_type=jnp.float32)
            left_ref[g, half * tok : (half + 1) * tok, :] = turned.astype(jnp.bfloat16)


def stack_input(input_blocks, groups, per):
    blocks, tok, lanes = input_blocks.shape
    rows = blocks * per
    return pl.pallas_call(
        stack_kernel,
        in_specs=[VMEM],
        out_specs=VMEM,
        out_shape=jax.ShapeDtypeStruct((groups, 2 * tok, rows), jnp.bfloat16),
        scratch_shapes=[pltpu.VMEM((groups, rows, tok), jnp.bfloat16)] * 2,
        compiler_params=pltpu.CompilerParams(vmem_limit_bytes=32 * 1024 * 1024),
        cost_estimate=pl.CostEstimate(
            flops=blocks * tok * lanes * 8, bytes_accessed=blocks * tok * lanes * 8, transcendentals=0
        ),
        name="stack_input",
    )(input_blocks)


def coded(value, most):
    exponent = jnp.floor(jnp.log2(jnp.maximum(most, SMALLEST)))
    v = value * jnp.exp2(-exponent)
    return v * jnp.abs(v) * CODE_UNIT, exponent


def decoded(code, exponent):
    code = code.astype(jnp.float32)
    value = jnp.sqrt(jnp.abs(code) * (1.0 / CODE_UNIT)) * jnp.exp2(exponent.astype(jnp.float32))
    return jnp.where(code < 0, -value, value)


def largest(value):
    return jnp.max(jnp.abs(value), axis=0, keepdims=True)


def conv_kernel(scale, lag_own, s_ref, left_ref, t_ref, out_ref, s_hi, s_lo, grads, cross, lag_sums):
    blocks, tok = 2 * s_ref.shape[0], left_ref.shape[1] // 2
    groups, rows, _ = grads.shape
    per = rows // blocks
    width = t_ref.shape[2]
    steps = width // tok
    used = min(steps, blocks)
    g = pl.program_id(0)

    @pl.when(g == 0)
    def _():
        s_hi[:, rows:, :] = jnp.zeros_like(s_hi[:, rows:, :])
        s_lo[:, rows:, :] = jnp.zeros_like(s_lo[:, rows:, :])
        for a in range(blocks):
            z, rest = divmod(a, blocks // 4)
            source, first = z // 2 * (blocks // 4) + rest, z % 2 * tok
            code, exponent = s_ref[source, first : first + tok, :], s_ref[source, 2 * tok : 2 * tok + 1, :]
            high, low = split(decoded(code, exponent).T[: groups * per])
            s_hi[:, a * per : (a + 1) * per, :] = high.reshape(groups, per, tok)
            s_lo[:, a * per : (a + 1) * per, :] = low.reshape(groups, per, tok)

    for d in range(0, used, 2):
        first, second = d * per, (d + 1) * per
        count = rows - first
        left = jnp.concatenate(
            [
                jnp.concatenate([ref[g, first : first + count, :], ref[g, second : second + count, :]], axis=1)
                for ref in (s_hi, s_lo)
            ],
            axis=0,
        )
        if d + 2 <= steps:
            right = t_ref[0, :, d * tok : (d + 2) * tok]
        else:
            right = jnp.concatenate([t_ref[0, :, d * tok :], jnp.zeros((2 * tok, tok), jnp.bfloat16)], axis=1)
        product = lax.dot_general(left, right, (((1,), (1,)), ((), ())), preferred_element_type=jnp.float32)
        term = product[:count, :tok] + (product[:count, tok:] + product[count:, :tok])
        if d == 0:
            grads[g] = term
        else:
            grads[g, :count, :] += term

    for d in range(0, used, 2):
        depth = min(rows, -(-(rows - d * per) // LANES) * LANES)
        high, low = [
            jnp.concatenate([ref[g, d * per : d * per + depth, :], ref[g, (d + 1) * per : (d + 1) * per + depth, :]], axis=1)
            for ref in (s_hi, s_lo)
        ]
        main = jnp.dot(left_ref[0, :, :depth], high, preferred_element_type=jnp.float32)
        rest = jnp.dot(left_ref[0, :tok, :depth], low, preferred_element_type=jnp.float32)
        stop = min(d + 2, steps)
        cross[:, d * tok : stop * tok] = (main[:tok] + (main[tok:] + rest))[:, : (stop - d) * tok]
    if used + used % 2 < steps:
        cross[:, (used + used % 2) * tok :] = jnp.zeros_like(cross[:, (used + used % 2) * tok :])
    skewed = pltpu.roll(cross[...], width - tok + 1, 1, stride=1, stride_axis=0)
    lag_sums[pl.ds(g, 1), :] = jnp.sum(skewed, axis=0, keepdims=True)[:, : width - tok] * scale

    @pl.when(g == groups - 1)
    def _():
        lags, lag_exponent = coded(lag_sums[...], largest(lag_sums[...]))
        held = out_ref.shape[1] - 8
        for a in range(blocks):
            out_ref[a, tok:held, :] = jnp.zeros_like(out_ref[a, tok:held, :])
            block = grads[:, a * per : (a + 1) * per, :].reshape(groups * per, tok).T
            code, exponent = coded(block, largest(block))
            if out_ref.shape[2] > groups * per:
                out_ref[a, :tok, :] = jnp.zeros_like(out_ref[a, :tok, :])
            out_ref[a, held:, :] = jnp.zeros_like(out_ref[a, held:, :])
            out_ref[a, :tok, : groups * per] = code
            out_ref[a, held : held + 1, : groups * per] = exponent
            own_lags = slice(a * lag_own, (a + 1) * lag_own)
            out_ref[a, tok : tok + groups, :lag_own] = lags[:, own_lags]
            out_ref[a, held + 1 : held + 2, :lag_own] = lag_exponent[:, own_lags]


def convolve(seq_blocks, input_blocks, moved, channels, lag_own, scale):
    blocks, tok, own = input_blocks.shape
    groups, _, width = moved.shape
    per = -(-channels // ROW_TILE) * ROW_TILE
    if groups * per != LANES or channels != per:
        wide = groups * per
        lanes = -(-wide // LANES) * LANES

        def widen(v):
            shape = v.shape[:-1]
            v = v.reshape(-1, groups, channels)
            v = jnp.pad(v, ((0, 0), (0, 0), (0, per - channels))).reshape(-1, wide)
            return jnp.pad(v, ((0, 0), (0, lanes - wide))).reshape(shape + (lanes,))

        seq_blocks, input_blocks = widen(seq_blocks), widen(input_blocks)
    rows = blocks * per
    left = stack_input(input_blocks, groups, per)
    extra = -(-(groups + 8) // ROW_TILE) * ROW_TILE
    out_lanes = max(groups * per, lag_own)
    return pl.pallas_call(
        functools.partial(conv_kernel, scale, lag_own),
        grid=(groups,),
        in_specs=[
            pl.BlockSpec(seq_blocks.shape, lambda g: (0, 0, 0)),
            pl.BlockSpec((1, 2 * tok, rows), lambda g: (g, 0, 0)),
            pl.BlockSpec((1, 2 * tok, width), lambda g: (g, 0, 0)),
        ],
        out_specs=pl.BlockSpec((blocks, tok + extra, out_lanes), lambda g: (0, 0, 0)),
        out_shape=jax.ShapeDtypeStruct((blocks, tok + extra, out_lanes), jnp.float32),
        scratch_shapes=[pltpu.VMEM((groups, 2 * rows, tok), jnp.bfloat16)] * 2
        + [
            pltpu.VMEM((groups, rows, tok), jnp.float32),
            pltpu.VMEM((tok, width), jnp.float32),
            pltpu.VMEM((groups, width - tok), jnp.float32),
        ],
        compiler_params=pltpu.CompilerParams(vmem_limit_bytes=48 * 1024 * 1024),
        cost_estimate=pl.CostEstimate(
            flops=groups * rows * tok * width * 14,
            bytes_accessed=12 * blocks * tok * LANES + 4 * groups * tok * width,
            transcendentals=0,
        ),
        name="convolve",
    )(seq_blocks, left, moved)


def nothing(*refs):
    del refs


def after(value, *earlier):
    return pl.pallas_call(
        nothing,
        in_specs=[ANY] * (1 + len(earlier)),
        out_specs=ANY,
        out_shape=jax.ShapeDtypeStruct(value.shape, value.dtype),
        input_output_aliases={0: 0},
        cost_estimate=pl.CostEstimate(flops=0, bytes_accessed=0, transcendentals=0),
        name="after",
    )(value, *earlier)


class Place:
    def __init__(self):
        self.devices = lax.axis_size("ctx")
        self.ys = self.devices // 8
        assert self.devices == 8 * self.ys
        me = lax.axis_index("ctx")
        self.core, chip = lax.rem(me, 2), me // 2
        self.y, z = lax.rem(chip, self.ys), chip // self.ys
        self.p, self.h = lax.rem(z, 2), z // 2
        self.block = (self.h * self.ys + self.y) * 2 + self.core

    def index(self, h, p, y, core):
        return ((h * 2 + p) * self.ys + y) * 2 + core

    def all(self):
        return [(h, p, y, c) for h in range(2) for p in range(2) for y in range(self.ys) for c in range(2)]

    def swap_core(self, v):
        return lax.ppermute(v, "ctx", [(self.index(h, p, y, c), self.index(h, p, y, 1 - c)) for h, p, y, c in self.all()])

    def swap_pair(self, v):
        return lax.ppermute(v, "ctx", [(self.index(h, p, y, c), self.index(h, 1 - p, y, c)) for h, p, y, c in self.all()])

    def swap_half(self, v):
        return lax.ppermute(v, "ctx", [(self.index(h, p, y, c), self.index(1 - h, p, y, c)) for h, p, y, c in self.all()])

    def swap_half_and_pair(self, v):
        pairs = [(self.index(h, p, y, c), self.index(1 - h, 1 - p, y, c)) for h, p, y, c in self.all()]
        return lax.ppermute(v, "ctx", pairs)

    def along_y(self, v, shift):
        ys = self.ys
        return lax.ppermute(
            v, "ctx", [(self.index(h, p, y, c), self.index(h, p, (y + shift) % ys, c)) for h, p, y, c in self.all()]
        )

    def same_p(self):
        return [[self.index(h, p, y, c) for h in range(2) for y in range(self.ys) for c in range(2)] for p in range(2)]


def pick_kernel(features, slots, core_ref, *refs):
    parts, (mine_ref, theirs_ref) = refs[: 2 * slots], refs[-2:]
    tok, held = parts[0].shape
    first = core_ref[0] == 0
    for row in range(2):
        rows = slice(row * tok, (row + 1) * tok)
        for s in range(slots):
            part = parts[row * slots + s]
            for b in range(held // (2 * features)):
                even = part[:, 2 * b * features : (2 * b + 1) * features]
                odd = part[:, (2 * b + 1) * features : (2 * b + 2) * features]
                at = s * held // 2 + b * features
                mine_ref[rows, at : at + features] = jnp.where(first, even, odd)
                theirs_ref[rows, at : at + features] = jnp.where(first, odd, even)


def gather_cotangent(cotangent, features, place, earlier):
    tok, held = cotangent.shape
    parts = lax.axis_size("ch")
    far = place.swap_pair(cotangent)

    def along_ch(v):
        return [v] + [lax.ppermute(v, "ch", [(j, (j + s) % parts) for j in range(parts)]) for s in range(1, parts)]

    whole = jax.ShapeDtypeStruct((2 * tok, parts * held // 2), cotangent.dtype)
    mine, theirs = pl.pallas_call(
        functools.partial(pick_kernel, features, parts),
        in_specs=[SMEM] + [VMEM] * (2 * parts),
        out_specs=[VMEM] * 2,
        out_shape=[whole, whole],
        compiler_params=pltpu.CompilerParams(vmem_limit_bytes=GRANT),
        cost_estimate=pl.CostEstimate(flops=0, bytes_accessed=8 * tok * held * parts, transcendentals=0),
        name="pick_features",
    )(place.core.reshape(1), *along_ch(cotangent), *along_ch(far))
    return mine, place.swap_core(after(theirs, *earlier))


def seq_kernel(p_ref, sum_ref, arrived_ref, gate_ref, far_gate_ref, *refs):
    out_ref, near_ref, far_ref = refs[-3:]
    p = p_ref[0]
    blocks, _, own = out_ref.shape
    tok = near_ref.shape[0]
    near_ref[...] = sum_ref[:tok, :] + arrived_ref[:tok, :]
    far_ref[...] = sum_ref[tok:, :] + arrived_ref[tok:, :]
    near = near_ref[...] * gate_ref[...]
    far = far_ref[...] * far_gate_ref[...]
    for b in range(blocks):
        here = slice(b * own, (b + 1) * own)
        most = jnp.maximum(largest(near[:, here]), largest(far[:, here]))
        for value, place in ((near, p), (far, 1 - p)):
            code, exponent = coded(value[:, here], most)
            out_ref[b, pl.ds(pl.multiple_of(place * tok, tok), tok), :] = code
        out_ref[b, 2 * tok :, :] = jnp.broadcast_to(exponent, (ROW_TILE, own))


def seq_blocks_of(total, arrived, gate_value, far_gate, place, *awaited):
    tok, channels = gate_value.shape
    blocks = place.devices // 2
    half = channels // 2
    own = half // blocks
    steps = max(1, min(4, half // LANES))
    width, count = half // steps, blocks // steps
    return pl.pallas_call(
        seq_kernel,
        grid_spec=pltpu.PrefetchScalarGridSpec(
            num_scalar_prefetch=1,
            grid=(steps,),
            in_specs=[
                pl.BlockSpec((2 * tok, width), lambda i, p: (0, i)),
                pl.BlockSpec((2 * tok, width), lambda i, p: (0, i)),
                pl.BlockSpec((tok, width), lambda i, p: (0, p[0] * steps + i)),
                pl.BlockSpec((tok, width), lambda i, p: (0, i)),
            ]
            + [ANY] * len(awaited),
            out_specs=[
                pl.BlockSpec((count, 2 * tok + ROW_TILE, own), lambda i, p: (i, 0, 0)),
                pl.BlockSpec((tok, width), lambda i, p: (0, i)),
                pl.BlockSpec((tok, width), lambda i, p: (0, i)),
            ],
        ),
        out_shape=[
            jax.ShapeDtypeStruct((blocks, 2 * tok + ROW_TILE, own), jnp.float32),
            jax.ShapeDtypeStruct((tok, half), jnp.float32),
            jax.ShapeDtypeStruct((tok, half), jnp.float32),
        ],
        compiler_params=pltpu.CompilerParams(vmem_limit_bytes=24 * 1024 * 1024),
        cost_estimate=pl.CostEstimate(
            flops=2 * tok * channels, bytes_accessed=24 * tok * channels, transcendentals=0
        ),
        name="seq_grad",
    )(place.p.reshape(1), total, arrived, gate_value, far_gate, *awaited)


def column_of(share, ctx, ch, ys, parts, features):
    other_h, other_p, shift = share
    chip = ctx // 2
    z, y = chip // ys, lax.rem(chip, ys)
    h, p = z // 2, lax.rem(z, 2)
    source = ((1 - h if other_h else h) * 2 + (1 - p if other_p else p)) * ys + lax.rem(y - shift + ys, ys)
    chips = 4 * ys // parts
    return (lax.rem(ch - source // chips + parts, parts) * chips + lax.rem(source, chips)) * features


def share_kernel(where, ys, parts, ctx_ref, ch_ref, mine_ref, theirs_ref, *refs):
    shares, before, (own_ref, other_ref) = refs[: len(where)], refs[len(where) : -2], refs[-2:]
    rows, features = mine_ref.shape[0], shares[0].shape[1]
    left = []
    for share in where:
        column = column_of(share, ctx_ref[0], ch_ref[0], ys, parts, features)
        at = pl.ds(pl.multiple_of(column, features), features)
        left.append(jnp.concatenate([mine_ref[:, at], theirs_ref[:, at]], axis=0))
    term = lax.dot_general(
        jnp.concatenate(left, axis=1),
        jnp.concatenate([share[...] for share in shares], axis=1),
        (((1,), (1,)), ((), ())),
        preferred_element_type=jnp.float32,
    )
    for i, ref in enumerate((own_ref, other_ref)):
        part = term[i * rows : (i + 1) * rows]
        ref[...] = part + before[i][...] if before else part


def add_shares(where, mine, theirs, shares, before, place):
    rows, (half, features) = mine.shape[0], shares[0].shape
    parts = lax.axis_size("ch")
    ctx, ch = lax.axis_index("ctx"), lax.axis_index("ch")
    if features % LANES:
        sums = list(before)
        for share, held in zip(where, shares):
            column = column_of(share, ctx, ch, place.ys, parts, features)
            terms = [
                lax.dot_general(
                    lax.dynamic_slice_in_dim(v, column, features, 1),
                    held,
                    (((1,), (1,)), ((), ())),
                    preferred_element_type=jnp.float32,
                )
                for v in (mine, theirs)
            ]
            sums = [a + b for a, b in zip(sums, terms)] if sums else terms
        return sums
    tile = min(256, half)
    whole = jax.ShapeDtypeStruct((rows, half), jnp.float32)
    tiles = pl.BlockSpec((rows, tile), lambda n: (0, n))
    return pl.pallas_call(
        functools.partial(share_kernel, where, place.ys, parts),
        grid=(half // tile,),
        in_specs=[SMEM] * 2
        + [pl.BlockSpec(mine.shape, lambda n: (0, 0))] * 2
        + [pl.BlockSpec((tile, features), lambda n: (n, 0))] * len(shares)
        + [tiles] * len(before),
        out_specs=[tiles] * 2,
        out_shape=[whole, whole],
        compiler_params=pltpu.CompilerParams(vmem_limit_bytes=GRANT),
        cost_estimate=pl.CostEstimate(
            flops=4 * rows * half * len(shares) * features,
            bytes_accessed=2 * (mine.size * 2 + half * len(shares) * features) + 16 * rows * half,
            transcendentals=0,
        ),
        name="add_shares",
    )(ctx.reshape(1), ch.reshape(1), mine, theirs, *shares, *before)


def project(cotangent, out_weight, place, *waited):
    channels, features = out_weight.shape
    half = channels // 2
    near = lax.dynamic_slice_in_dim(out_weight, place.p * half, half, 0)
    given = lax.dynamic_slice_in_dim(out_weight, (1 - place.p) * half, half, 0)
    far = place.swap_half(near)
    paired = place.swap_pair(given)
    far_paired = place.swap_half_and_pair(after(given, far))

    def along_y(v):
        return [v] + [place.along_y(v, shift) for shift in range(1, place.ys)]

    held = [along_y(near)]
    held.append(along_y(after(paired, *held[0][1:])))
    held.append(along_y(far))
    held.append(along_y(after(far_paired, *held[1][1:], *held[2][1:])))
    mine, theirs = gather_cotangent(cotangent, features, place, [*held[3][1:], *waited])
    shares = [
        ((other // 2, other % 2, shift), held[other][shift]) for other in range(4) for shift in range(place.ys)
    ]
    sums = []
    for some in (shares,):
        sums = add_shares([at for at, _ in some], mine, theirs, [v for _, v in some], sums, place)
    own, other = sums
    return own, place.swap_core(other), far_paired


def code_kernel(x_ref, *refs):
    out_ref = refs[-1]
    devices, rows, own = out_ref.shape
    tok = x_ref.shape[0]
    code, exponent = coded(x_ref[...], largest(x_ref[...]))
    quarter = devices // 4
    for i in range(devices):
        h, p, rest = i // (2 * quarter), i // quarter % 2, i % quarter
        block = (p * 2 + h) * quarter + rest
        out_ref[i, :tok, :] = code[:, block * own : (block + 1) * own]
        out_ref[i, tok:, :] = jnp.broadcast_to(exponent[:, block * own : (block + 1) * own], (rows - tok, own))


def code_blocks(value, devices, *awaited):
    tok, channels = value.shape
    return pl.pallas_call(
        code_kernel,
        in_specs=[VMEM] + [ANY] * len(awaited),
        out_specs=VMEM,
        out_shape=jax.ShapeDtypeStruct((devices, tok + ROW_TILE, channels // devices), jnp.float32),
        compiler_params=pltpu.CompilerParams(vmem_limit_bytes=32 * 1024 * 1024),
        cost_estimate=pl.CostEstimate(flops=4 * tok * channels, bytes_accessed=8 * tok * channels, transcendentals=0),
        name="code_input",
    )(value, *awaited)


def body(cotangent, out_weight, gate_value, conv_output, conv_input, filters):
    tok, channels = gate_value.shape
    all_groups, lags = filters.shape
    place = Place()
    devices = place.devices
    per_group = channels // all_groups
    own = channels // devices
    half = channels // 2
    groups = max(1, own // per_group)
    share = max(1, per_group // own)
    lag_own = lags // devices

    def exchange(blocks, groups=None):
        return lax.all_to_all(blocks, "ctx", 0, 0, tiled=True, axis_index_groups=groups)

    def reorder(blocks):
        return blocks.reshape((2, 2, devices // 4) + blocks.shape[1:]).swapaxes(0, 1).reshape(blocks.shape)

    far_gate = place.swap_pair(lax.dynamic_slice_in_dim(gate_value, (1 - place.p) * half, half, 1))
    total, arrived, late = project(cotangent, out_weight, place, far_gate)
    code = exchange(code_blocks(conv_input, devices, late).astype(jnp.float16))
    input_blocks = decoded(code[:, :tok], code[:, tok : tok + 1])
    first_group = (place.p * half + place.block * own) // per_group
    moved = toeplitz(lax.dynamic_slice_in_dim(filters, first_group, groups, 0), tok)

    seq_code, near, far = seq_blocks_of(total, arrived, gate_value, far_gate, place)
    seq_code = exchange(seq_code.astype(jnp.float16), place.same_p())
    seq_blocks = seq_code.astype(jnp.float32)
    far = place.swap_pair(far)
    left = jnp.where(place.p == 0, near, far)
    right = jnp.where(place.p == 0, far, near)
    gate_grad = jnp.concatenate([left, right], axis=1) * conv_output

    scale = 1.0 / math.sqrt(per_group * tok * devices)
    result = convolve(seq_blocks, input_blocks, moved, min(own, per_group), lag_own, scale)
    back = exchange(result[:, :, : max(own, lag_own)].astype(jnp.float16))
    held = back.shape[1] - 8
    input_grad = reorder(decoded(back[:, :tok, :own], back[:, held : held + 1, :own]))
    input_grad = input_grad.transpose(1, 0, 2).reshape(tok, channels)
    filter_grad = reorder(decoded(back[:, tok : tok + groups, :lag_own], back[:, held + 1 : held + 2, :lag_own]))
    filter_grad = filter_grad.reshape(all_groups, share, lag_own).sum(axis=1)
    return (input_grad, gate_grad, filter_grad)


def solution(mesh):
    return jax.shard_map(
        body,
        mesh=mesh,
        in_specs=(
            P("ctx", "ch"),
            P("ch", "ctx"),
            P("ctx", "ch"),
            P("ctx", "ch"),
            P("ctx", "ch"),
            P("ch", None),
        ),
        out_specs=(P("ctx", "ch"), P("ctx", "ch"), P("ch", "ctx")),
        check_vma=False,
    )
```

```python
import functools
import math

import jax
import jax.numpy as jnp
from jax import lax
from jax.experimental import pallas as pl
from jax.experimental.pallas import tpu as pltpu
from jax.sharding import PartitionSpec as P

LANES = 128
ROW_TILE = 16
GRANT = 60 * 1024 * 1024
CODE_UNIT = 8192.0
SMALLEST = 1e-30
VMEM = pl.BlockSpec(memory_space=pltpu.VMEM)
SMEM = pl.BlockSpec(memory_space=pltpu.SMEM)
ANY = pl.BlockSpec(memory_space=pl.ANY)


def split(value):
    high = value.astype(jnp.bfloat16)
    return high, (value - high.astype(jnp.float32)).astype(jnp.bfloat16)


def toeplitz_kernel(filter_ref, out_ref):
    tok = out_ref.shape[1] // 2
    rows = jnp.broadcast_to(filter_ref[0], (tok, filter_ref.shape[2]))
    high, low = split(pltpu.roll(rows, 0, 1, stride=1, stride_axis=0))
    out_ref[0, :tok, :] = high
    out_ref[0, tok:, :] = low


def toeplitz(filters, tok):
    groups, lags = filters.shape
    width = lags + tok
    padded = jnp.pad(filters, ((0, 0), (0, tok)))[:, None, :]
    return pl.pallas_call(
        toeplitz_kernel,
        grid=(groups,),
        in_specs=[pl.BlockSpec((1, 1, width), lambda g: (g, 0, 0))],
        out_specs=pl.BlockSpec((1, 2 * tok, width), lambda g: (g, 0, 0)),
        out_shape=jax.ShapeDtypeStruct((groups, 2 * tok, width), jnp.bfloat16),
        cost_estimate=pl.CostEstimate(
            flops=groups * tok * width * 4, bytes_accessed=groups * width * (4 + 4 * tok), transcendentals=0
        ),
        name="toeplitz",
    )(padded)


def stack_kernel(x_ref, left_ref, x_hi, x_lo):
    blocks, tok, _ = x_ref.shape
    groups, rows, _ = x_hi.shape
    per = rows // blocks

    @pl.loop(0, blocks)
    def _(a):
        at = pl.ds(pl.multiple_of(a * per, per), per)
        high, low = split(x_ref[a].T[: groups * per])
        x_hi[:, at, :] = high.reshape(groups, per, tok)
        x_lo[:, at, :] = low.reshape(groups, per, tok)

    last = lax.broadcasted_iota(jnp.int32, (tok, tok), 0) + lax.broadcasted_iota(jnp.int32, (tok, tok), 1)
    turn = jnp.where(last == tok - 1, 1.0, 0.0).astype(jnp.bfloat16)

    @pl.loop(0, groups)
    def _(g):
        for half, ref in ((0, x_hi), (1, x_lo)):
            turned = lax.dot_general(turn, ref[g], (((1,), (1,)), ((), ())), preferred_element_type=jnp.float32)
            left_ref[g, half * tok : (half + 1) * tok, :] = turned.astype(jnp.bfloat16)


def stack_input(input_blocks, groups, per):
    blocks, tok, lanes = input_blocks.shape
    rows = blocks * per
    return pl.pallas_call(
        stack_kernel,
        in_specs=[VMEM],
        out_specs=VMEM,
        out_shape=jax.ShapeDtypeStruct((groups, 2 * tok, rows), jnp.bfloat16),
        scratch_shapes=[pltpu.VMEM((groups, rows, tok), jnp.bfloat16)] * 2,
        compiler_params=pltpu.CompilerParams(vmem_limit_bytes=32 * 1024 * 1024),
        cost_estimate=pl.CostEstimate(
            flops=blocks * tok * lanes * 8, bytes_accessed=blocks * tok * lanes * 8, transcendentals=0
        ),
        name="stack_input",
    )(input_blocks)


def coded(value, most):
    exponent = jnp.floor(jnp.log2(jnp.maximum(most, SMALLEST)))
    v = value * jnp.exp2(-exponent)
    return v * jnp.abs(v) * CODE_UNIT, exponent


def decoded(code, exponent):
    code = code.astype(jnp.float32)
    value = jnp.sqrt(jnp.abs(code) * (1.0 / CODE_UNIT)) * jnp.exp2(exponent.astype(jnp.float32))
    return jnp.where(code < 0, -value, value)


def largest(value):
    return jnp.max(jnp.abs(value), axis=0, keepdims=True)


def conv_kernel(scale, lag_own, s_ref, left_ref, t_ref, out_ref, s_hi, s_lo, grads, cross, lag_sums):
    blocks, tok = 2 * s_ref.shape[0], left_ref.shape[1] // 2
    groups, rows, _ = grads.shape
    per = rows // blocks
    width = t_ref.shape[2]
    steps = width // tok
    used = min(steps, blocks)
    g = pl.program_id(0)

    @pl.when(g == 0)
    def _():
        s_hi[:, rows:, :] = jnp.zeros_like(s_hi[:, rows:, :])
        s_lo[:, rows:, :] = jnp.zeros_like(s_lo[:, rows:, :])
        for a in range(blocks):
            z, rest = divmod(a, blocks // 4)
            source, first = z // 2 * (blocks // 4) + rest, z % 2 * tok
            code, exponent = s_ref[source, first : first + tok, :], s_ref[source, 2 * tok : 2 * tok + 1, :]
            high, low = split(decoded(code, exponent).T[: groups * per])
            s_hi[:, a * per : (a + 1) * per, :] = high.reshape(groups, per, tok)
            s_lo[:, a * per : (a + 1) * per, :] = low.reshape(groups, per, tok)

    for d in range(0, used, 2):
        first, second = d * per, (d + 1) * per
        count = rows - first
        left = jnp.concatenate(
            [
                jnp.concatenate([ref[g, first : first + count, :], ref[g, second : second + count, :]], axis=1)
                for ref in (s_hi, s_lo)
            ],
            axis=0,
        )
        if d + 2 <= steps:
            right = t_ref[0, :, d * tok : (d + 2) * tok]
        else:
            right = jnp.concatenate([t_ref[0, :, d * tok :], jnp.zeros((2 * tok, tok), jnp.bfloat16)], axis=1)
        product = lax.dot_general(left, right, (((1,), (1,)), ((), ())), preferred_element_type=jnp.float32)
        term = product[:count, :tok] + (product[:count, tok:] + product[count:, :tok])
        if d == 0:
            grads[g] = term
        else:
            grads[g, :count, :] += term

    for d in range(0, used, 2):
        depth = min(rows, -(-(rows - d * per) // LANES) * LANES)
        high, low = [
            jnp.concatenate([ref[g, d * per : d * per + depth, :], ref[g, (d + 1) * per : (d + 1) * per + depth, :]], axis=1)
            for ref in (s_hi, s_lo)
        ]
        main = jnp.dot(left_ref[0, :, :depth], high, preferred_element_type=jnp.float32)
        rest = jnp.dot(left_ref[0, :tok, :depth], low, preferred_element_type=jnp.float32)
        stop = min(d + 2, steps)
        cross[:, d * tok : stop * tok] = (main[:tok] + (main[tok:] + rest))[:, : (stop - d) * tok]
    if used + used % 2 < steps:
        cross[:, (used + used % 2) * tok :] = jnp.zeros_like(cross[:, (used + used % 2) * tok :])
    skewed = pltpu.roll(cross[...], width - tok + 1, 1, stride=1, stride_axis=0)
    lag_sums[pl.ds(g, 1), :] = jnp.sum(skewed, axis=0, keepdims=True)[:, : width - tok] * scale

    @pl.when(g == groups - 1)
    def _():
        lags, lag_exponent = coded(lag_sums[...], largest(lag_sums[...]))
        held = out_ref.shape[1] - 8
        for a in range(blocks):
            out_ref[a, tok:held, :] = jnp.zeros_like(out_ref[a, tok:held, :])
            block = grads[:, a * per : (a + 1) * per, :].reshape(groups * per, tok).T
            code, exponent = coded(block, largest(block))
            if out_ref.shape[2] > groups * per:
                out_ref[a, :tok, :] = jnp.zeros_like(out_ref[a, :tok, :])
            out_ref[a, held:, :] = jnp.zeros_like(out_ref[a, held:, :])
            out_ref[a, :tok, : groups * per] = code
            out_ref[a, held : held + 1, : groups * per] = exponent
            own_lags = slice(a * lag_own, (a + 1) * lag_own)
            out_ref[a, tok : tok + groups, :lag_own] = lags[:, own_lags]
            out_ref[a, held + 1 : held + 2, :lag_own] = lag_exponent[:, own_lags]


def convolve(seq_blocks, input_blocks, moved, channels, lag_own, scale):
    blocks, tok, own = input_blocks.shape
    groups, _, width = moved.shape
    per = -(-channels // ROW_TILE) * ROW_TILE
    if groups * per != LANES or channels != per:
        wide = groups * per
        lanes = -(-wide // LANES) * LANES

        def widen(v):
            shape = v.shape[:-1]
            v = v.reshape(-1, groups, channels)
            v = jnp.pad(v, ((0, 0), (0, 0), (0, per - channels))).reshape(-1, wide)
            return jnp.pad(v, ((0, 0), (0, lanes - wide))).reshape(shape + (lanes,))

        seq_blocks, input_blocks = widen(seq_blocks), widen(input_blocks)
    rows = blocks * per
    left = stack_input(input_blocks, groups, per)
    extra = -(-(groups + 8) // ROW_TILE) * ROW_TILE
    out_lanes = max(groups * per, lag_own)
    return pl.pallas_call(
        functools.partial(conv_kernel, scale, lag_own),
        grid=(groups,),
        in_specs=[
            pl.BlockSpec(seq_blocks.shape, lambda g: (0, 0, 0)),
            pl.BlockSpec((1, 2 * tok, rows), lambda g: (g, 0, 0)),
            pl.BlockSpec((1, 2 * tok, width), lambda g: (g, 0, 0)),
        ],
        out_specs=pl.BlockSpec((blocks, tok + extra, out_lanes), lambda g: (0, 0, 0)),
        out_shape=jax.ShapeDtypeStruct((blocks, tok + extra, out_lanes), jnp.float32),
        scratch_shapes=[pltpu.VMEM((groups, 2 * rows, tok), jnp.bfloat16)] * 2
        + [
            pltpu.VMEM((groups, rows, tok), jnp.float32),
            pltpu.VMEM((tok, width), jnp.float32),
            pltpu.VMEM((groups, width - tok), jnp.float32),
        ],
        compiler_params=pltpu.CompilerParams(vmem_limit_bytes=48 * 1024 * 1024),
        cost_estimate=pl.CostEstimate(
            flops=groups * rows * tok * width * 14,
            bytes_accessed=12 * blocks * tok * LANES + 4 * groups * tok * width,
            transcendentals=0,
        ),
        name="convolve",
    )(seq_blocks, left, moved)


def nothing(*refs):
    del refs


def after(value, *earlier):
    return pl.pallas_call(
        nothing,
        in_specs=[ANY] * (1 + len(earlier)),
        out_specs=ANY,
        out_shape=jax.ShapeDtypeStruct(value.shape, value.dtype),
        input_output_aliases={0: 0},
        cost_estimate=pl.CostEstimate(flops=0, bytes_accessed=0, transcendentals=0),
        name="after",
    )(value, *earlier)


class Place:
    def __init__(self):
        self.devices = lax.axis_size("ctx")
        self.ys = self.devices // 8
        assert self.devices == 8 * self.ys
        me = lax.axis_index("ctx")
        self.core, chip = lax.rem(me, 2), me // 2
        self.y, z = lax.rem(chip, self.ys), chip // self.ys
        self.p, self.h = lax.rem(z, 2), z // 2
        self.block = (self.h * self.ys + self.y) * 2 + self.core

    def index(self, h, p, y, core):
        return ((h * 2 + p) * self.ys + y) * 2 + core

    def all(self):
        return [(h, p, y, c) for h in range(2) for p in range(2) for y in range(self.ys) for c in range(2)]

    def swap_core(self, v):
        return lax.ppermute(v, "ctx", [(self.index(h, p, y, c), self.index(h, p, y, 1 - c)) for h, p, y, c in self.all()])

    def swap_pair(self, v):
        return lax.ppermute(v, "ctx", [(self.index(h, p, y, c), self.index(h, 1 - p, y, c)) for h, p, y, c in self.all()])

    def swap_half(self, v):
        return lax.ppermute(v, "ctx", [(self.index(h, p, y, c), self.index(1 - h, p, y, c)) for h, p, y, c in self.all()])

    def swap_half_and_pair(self, v):
        pairs = [(self.index(h, p, y, c), self.index(1 - h, 1 - p, y, c)) for h, p, y, c in self.all()]
        return lax.ppermute(v, "ctx", pairs)

    def along_y(self, v, shift):
        ys = self.ys
        return lax.ppermute(
            v, "ctx", [(self.index(h, p, y, c), self.index(h, p, (y + shift) % ys, c)) for h, p, y, c in self.all()]
        )

    def same_p(self):
        return [[self.index(h, p, y, c) for h in range(2) for y in range(self.ys) for c in range(2)] for p in range(2)]


def pick_kernel(features, slots, core_ref, *refs):
    parts, (mine_ref, theirs_ref) = refs[: 2 * slots], refs[-2:]
    tok, held = parts[0].shape
    first = core_ref[0] == 0
    for row in range(2):
        rows = slice(row * tok, (row + 1) * tok)
        for s in range(slots):
            part = parts[row * slots + s]
            for b in range(held // (2 * features)):
                even = part[:, 2 * b * features : (2 * b + 1) * features]
                odd = part[:, (2 * b + 1) * features : (2 * b + 2) * features]
                at = s * held // 2 + b * features
                mine_ref[rows, at : at + features] = jnp.where(first, even, odd)
                theirs_ref[rows, at : at + features] = jnp.where(first, odd, even)


def gather_cotangent(cotangent, features, place, earlier):
    tok, held = cotangent.shape
    parts = lax.axis_size("ch")
    far = place.swap_pair(cotangent)

    def along_ch(v):
        return [v] + [lax.ppermute(v, "ch", [(j, (j + s) % parts) for j in range(parts)]) for s in range(1, parts)]

    whole = jax.ShapeDtypeStruct((2 * tok, parts * held // 2), cotangent.dtype)
    mine, theirs = pl.pallas_call(
        functools.partial(pick_kernel, features, parts),
        in_specs=[SMEM] + [VMEM] * (2 * parts),
        out_specs=[VMEM] * 2,
        out_shape=[whole, whole],
        compiler_params=pltpu.CompilerParams(vmem_limit_bytes=GRANT),
        cost_estimate=pl.CostEstimate(flops=0, bytes_accessed=8 * tok * held * parts, transcendentals=0),
        name="pick_features",
    )(place.core.reshape(1), *along_ch(cotangent), *along_ch(far))
    return mine, place.swap_core(after(theirs, *earlier))


def seq_kernel(p_ref, sum_ref, arrived_ref, gate_ref, far_gate_ref, *refs):
    out_ref, near_ref, far_ref = refs[-3:]
    p = p_ref[0]
    blocks, _, own = out_ref.shape
    tok = near_ref.shape[0]
    near_ref[...] = sum_ref[:tok, :] + arrived_ref[:tok, :]
    far_ref[...] = sum_ref[tok:, :] + arrived_ref[tok:, :]
    near = near_ref[...] * gate_ref[...]
    far = far_ref[...] * far_gate_ref[...]
    for b in range(blocks):
        here = slice(b * own, (b + 1) * own)
        most = jnp.maximum(largest(near[:, here]), largest(far[:, here]))
        for value, place in ((near, p), (far, 1 - p)):
            code, exponent = coded(value[:, here], most)
            out_ref[b, pl.ds(pl.multiple_of(place * tok, tok), tok), :] = code
        out_ref[b, 2 * tok :, :] = jnp.broadcast_to(exponent, (ROW_TILE, own))


def seq_blocks_of(total, arrived, gate_value, far_gate, place, *awaited):
    tok, channels = gate_value.shape
    blocks = place.devices // 2
    half = channels // 2
    own = half // blocks
    steps = max(1, min(4, half // LANES))
    width, count = half // steps, blocks // steps
    return pl.pallas_call(
        seq_kernel,
        grid_spec=pltpu.PrefetchScalarGridSpec(
            num_scalar_prefetch=1,
            grid=(steps,),
            in_specs=[
                pl.BlockSpec((2 * tok, width), lambda i, p: (0, i)),
                pl.BlockSpec((2 * tok, width), lambda i, p: (0, i)),
                pl.BlockSpec((tok, width), lambda i, p: (0, p[0] * steps + i)),
                pl.BlockSpec((tok, width), lambda i, p: (0, i)),
            ]
            + [ANY] * len(awaited),
            out_specs=[
                pl.BlockSpec((count, 2 * tok + ROW_TILE, own), lambda i, p: (i, 0, 0)),
                pl.BlockSpec((tok, width), lambda i, p: (0, i)),
                pl.BlockSpec((tok, width), lambda i, p: (0, i)),
            ],
        ),
        out_shape=[
            jax.ShapeDtypeStruct((blocks, 2 * tok + ROW_TILE, own), jnp.float32),
            jax.ShapeDtypeStruct((tok, half), jnp.float32),
            jax.ShapeDtypeStruct((tok, half), jnp.float32),
        ],
        compiler_params=pltpu.CompilerParams(vmem_limit_bytes=24 * 1024 * 1024),
        cost_estimate=pl.CostEstimate(
            flops=2 * tok * channels, bytes_accessed=24 * tok * channels, transcendentals=0
        ),
        name="seq_grad",
    )(place.p.reshape(1), total, arrived, gate_value, far_gate, *awaited)


def column_of(share, ctx, ch, ys, parts, features):
    other_h, other_p, shift = share
    chip = ctx // 2
    z, y = chip // ys, lax.rem(chip, ys)
    h, p = z // 2, lax.rem(z, 2)
    source = ((1 - h if other_h else h) * 2 + (1 - p if other_p else p)) * ys + lax.rem(y - shift + ys, ys)
    chips = 4 * ys // parts
    return (lax.rem(ch - source // chips + parts, parts) * chips + lax.rem(source, chips)) * features


def share_kernel(where, ys, parts, ctx_ref, ch_ref, mine_ref, theirs_ref, *refs):
    shares, before, (own_ref, other_ref) = refs[: len(where)], refs[len(where) : -2], refs[-2:]
    rows, features = mine_ref.shape[0], shares[0].shape[1]
    left = []
    for share in where:
        column = column_of(share, ctx_ref[0], ch_ref[0], ys, parts, features)
        at = pl.ds(pl.multiple_of(column, features), features)
        left.append(jnp.concatenate([mine_ref[:, at], theirs_ref[:, at]], axis=0))
    term = lax.dot_general(
        jnp.concatenate(left, axis=1),
        jnp.concatenate([share[...] for share in shares], axis=1),
        (((1,), (1,)), ((), ())),
        preferred_element_type=jnp.float32,
    )
    for i, ref in enumerate((own_ref, other_ref)):
        part = term[i * rows : (i + 1) * rows]
        ref[...] = part + before[i][...] if before else part


def add_shares(where, mine, theirs, shares, before, place):
    rows, (half, features) = mine.shape[0], shares[0].shape
    parts = lax.axis_size("ch")
    ctx, ch = lax.axis_index("ctx"), lax.axis_index("ch")
    if features % LANES:
        sums = list(before)
        for share, held in zip(where, shares):
            column = column_of(share, ctx, ch, place.ys, parts, features)
            terms = [
                lax.dot_general(
                    lax.dynamic_slice_in_dim(v, column, features, 1),
                    held,
                    (((1,), (1,)), ((), ())),
                    preferred_element_type=jnp.float32,
                )
                for v in (mine, theirs)
            ]
            sums = [a + b for a, b in zip(sums, terms)] if sums else terms
        return sums
    tile = min(256, half)
    whole = jax.ShapeDtypeStruct((rows, half), jnp.float32)
    tiles = pl.BlockSpec((rows, tile), lambda n: (0, n))
    return pl.pallas_call(
        functools.partial(share_kernel, where, place.ys, parts),
        grid=(half // tile,),
        in_specs=[SMEM] * 2
        + [pl.BlockSpec(mine.shape, lambda n: (0, 0))] * 2
        + [pl.BlockSpec((tile, features), lambda n: (n, 0))] * len(shares)
        + [tiles] * len(before),
        out_specs=[tiles] * 2,
        out_shape=[whole, whole],
        compiler_params=pltpu.CompilerParams(vmem_limit_bytes=GRANT),
        cost_estimate=pl.CostEstimate(
            flops=4 * rows * half * len(shares) * features,
            bytes_accessed=2 * (mine.size * 2 + half * len(shares) * features) + 16 * rows * half,
            transcendentals=0,
        ),
        name="add_shares",
    )(ctx.reshape(1), ch.reshape(1), mine, theirs, *shares, *before)


def project(cotangent, out_weight, place, waited, between):
    channels, features = out_weight.shape
    half = channels // 2
    near = lax.dynamic_slice_in_dim(out_weight, place.p * half, half, 0)
    given = lax.dynamic_slice_in_dim(out_weight, (1 - place.p) * half, half, 0)
    far = place.swap_half(near)
    paired = place.swap_pair(given)
    far_paired = place.swap_half_and_pair(after(given, far))

    def along_y(v):
        return [v] + [place.along_y(v, shift) for shift in range(1, place.ys)]

    held = [along_y(near)]
    held.append(along_y(after(paired, *held[0][1:])))
    held.append(along_y(far))
    held.append(along_y(after(far_paired, *held[1][1:], *held[2][1:])))
    made = between(held[2][-1])
    mine, theirs = gather_cotangent(cotangent, features, place, [*held[3][1:], waited, made])
    shares = [
        ((other // 2, other % 2, shift), held[other][shift]) for other in range(4) for shift in range(place.ys)
    ]
    sums = []
    for some in (shares,):
        sums = add_shares([at for at, _ in some], mine, theirs, [v for _, v in some], sums, place)
    own, other = sums
    return own, place.swap_core(other), made


def code_kernel(x_ref, *refs):
    out_ref = refs[-1]
    devices, rows, own = out_ref.shape
    tok = x_ref.shape[0]
    code, exponent = coded(x_ref[...], largest(x_ref[...]))
    quarter = devices // 4
    for i in range(devices):
        h, p, rest = i // (2 * quarter), i // quarter % 2, i % quarter
        block = (p * 2 + h) * quarter + rest
        out_ref[i, :tok, :] = code[:, block * own : (block + 1) * own]
        out_ref[i, tok:, :] = jnp.broadcast_to(exponent[:, block * own : (block + 1) * own], (rows - tok, own))


def code_blocks(value, devices, *awaited):
    tok, channels = value.shape
    return pl.pallas_call(
        code_kernel,
        in_specs=[VMEM] + [ANY] * len(awaited),
        out_specs=VMEM,
        out_shape=jax.ShapeDtypeStruct((devices, tok + ROW_TILE, channels // devices), jnp.float32),
        compiler_params=pltpu.CompilerParams(vmem_limit_bytes=32 * 1024 * 1024),
        cost_estimate=pl.CostEstimate(flops=4 * tok * channels, bytes_accessed=8 * tok * channels, transcendentals=0),
        name="code_input",
    )(value, *awaited)


def body(cotangent, out_weight, gate_value, conv_output, conv_input, filters):
    tok, channels = gate_value.shape
    all_groups, lags = filters.shape
    place = Place()
    devices = place.devices
    per_group = channels // all_groups
    own = channels // devices
    half = channels // 2
    groups = max(1, own // per_group)
    share = max(1, per_group // own)
    lag_own = lags // devices

    def exchange(blocks, groups=None):
        return lax.all_to_all(blocks, "ctx", 0, 0, tiled=True, axis_index_groups=groups)

    def reorder(blocks):
        return blocks.reshape((2, 2, devices // 4) + blocks.shape[1:]).swapaxes(0, 1).reshape(blocks.shape)

    far_gate = place.swap_pair(lax.dynamic_slice_in_dim(gate_value, (1 - place.p) * half, half, 1))
    total, arrived, code = project(
        cotangent, out_weight, place, far_gate, lambda earlier: code_blocks(conv_input, devices, earlier)
    )
    code = exchange(code.astype(jnp.float16))
    input_blocks = decoded(code[:, :tok], code[:, tok : tok + 1])
    first_group = (place.p * half + place.block * own) // per_group
    moved = toeplitz(lax.dynamic_slice_in_dim(filters, first_group, groups, 0), tok)

    seq_code, near, far = seq_blocks_of(total, arrived, gate_value, far_gate, place)
    seq_code = exchange(seq_code.astype(jnp.float16), place.same_p())
    seq_blocks = seq_code.astype(jnp.float32)
    far = place.swap_pair(far)
    left = jnp.where(place.p == 0, near, far)
    right = jnp.where(place.p == 0, far, near)
    gate_grad = jnp.concatenate([left, right], axis=1) * conv_output

    scale = 1.0 / math.sqrt(per_group * tok * devices)
    result = convolve(seq_blocks, input_blocks, moved, min(own, per_group), lag_own, scale)
    back = exchange(result[:, :, : max(own, lag_own)].astype(jnp.float16))
    held = back.shape[1] - 8
    input_grad = reorder(decoded(back[:, :tok, :own], back[:, held : held + 1, :own]))
    input_grad = input_grad.transpose(1, 0, 2).reshape(tok, channels)
    filter_grad = reorder(decoded(back[:, tok : tok + groups, :lag_own], back[:, held + 1 : held + 2, :lag_own]))
    filter_grad = filter_grad.reshape(all_groups, share, lag_own).sum(axis=1)
    return (input_grad, gate_grad, filter_grad)


def solution(mesh):
    return jax.shard_map(
        body,
        mesh=mesh,
        in_specs=(
            P("ctx", "ch"),
            P("ch", "ctx"),
            P("ctx", "ch"),
            P("ctx", "ch"),
            P("ctx", "ch"),
            P("ch", None),
        ),
        out_specs=(P("ctx", "ch"), P("ctx", "ch"), P("ch", "ctx")),
        check_vma=False,
    )
```

```python
import functools
import math

import jax
import jax.numpy as jnp
from jax import lax
from jax.experimental import pallas as pl
from jax.experimental.pallas import tpu as pltpu
from jax.sharding import PartitionSpec as P

LANES = 128
ROW_TILE = 16
GRANT = 60 * 1024 * 1024
CODE_UNIT = 8192.0
SMALLEST = 1e-30
VMEM = pl.BlockSpec(memory_space=pltpu.VMEM)
SMEM = pl.BlockSpec(memory_space=pltpu.SMEM)
ANY = pl.BlockSpec(memory_space=pl.ANY)


def split(value):
    high = value.astype(jnp.bfloat16)
    return high, (value - high.astype(jnp.float32)).astype(jnp.bfloat16)


def toeplitz_kernel(filter_ref, out_ref):
    tok = out_ref.shape[1] // 2
    rows = jnp.broadcast_to(filter_ref[0], (tok, filter_ref.shape[2]))
    high, low = split(pltpu.roll(rows, 0, 1, stride=1, stride_axis=0))
    out_ref[0, :tok, :] = high
    out_ref[0, tok:, :] = low


def toeplitz(filters, tok):
    groups, lags = filters.shape
    width = lags + tok
    padded = jnp.pad(filters, ((0, 0), (0, tok)))[:, None, :]
    return pl.pallas_call(
        toeplitz_kernel,
        grid=(groups,),
        in_specs=[pl.BlockSpec((1, 1, width), lambda g: (g, 0, 0))],
        out_specs=pl.BlockSpec((1, 2 * tok, width), lambda g: (g, 0, 0)),
        out_shape=jax.ShapeDtypeStruct((groups, 2 * tok, width), jnp.bfloat16),
        cost_estimate=pl.CostEstimate(
            flops=groups * tok * width * 4, bytes_accessed=groups * width * (4 + 4 * tok), transcendentals=0
        ),
        name="toeplitz",
    )(padded)


def stack_kernel(x_ref, left_ref, x_hi, x_lo):
    blocks, tok, _ = x_ref.shape
    groups, rows, _ = x_hi.shape
    per = rows // blocks

    @pl.loop(0, blocks)
    def _(a):
        at = pl.ds(pl.multiple_of(a * per, per), per)
        high, low = split(x_ref[a].T[: groups * per])
        x_hi[:, at, :] = high.reshape(groups, per, tok)
        x_lo[:, at, :] = low.reshape(groups, per, tok)

    last = lax.broadcasted_iota(jnp.int32, (tok, tok), 0) + lax.broadcasted_iota(jnp.int32, (tok, tok), 1)
    turn = jnp.where(last == tok - 1, 1.0, 0.0).astype(jnp.bfloat16)

    @pl.loop(0, groups)
    def _(g):
        for half, ref in ((0, x_hi), (1, x_lo)):
            turned = lax.dot_general(turn, ref[g], (((1,), (1,)), ((), ())), preferred_element_type=jnp.float32)
            left_ref[g, half * tok : (half + 1) * tok, :] = turned.astype(jnp.bfloat16)


def stack_input(input_blocks, groups, per):
    blocks, tok, lanes = input_blocks.shape
    rows = blocks * per
    return pl.pallas_call(
        stack_kernel,
        in_specs=[VMEM],
        out_specs=VMEM,
        out_shape=jax.ShapeDtypeStruct((groups, 2 * tok, rows), jnp.bfloat16),
        scratch_shapes=[pltpu.VMEM((groups, rows, tok), jnp.bfloat16)] * 2,
        compiler_params=pltpu.CompilerParams(vmem_limit_bytes=32 * 1024 * 1024),
        cost_estimate=pl.CostEstimate(
            flops=blocks * tok * lanes * 8, bytes_accessed=blocks * tok * lanes * 8, transcendentals=0
        ),
        name="stack_input",
    )(input_blocks)


def coded(value, most):
    exponent = jnp.floor(jnp.log2(jnp.maximum(most, SMALLEST)))
    v = value * jnp.exp2(-exponent)
    return v * jnp.abs(v) * CODE_UNIT, exponent


def decoded(code, exponent):
    code = code.astype(jnp.float32)
    value = jnp.sqrt(jnp.abs(code) * (1.0 / CODE_UNIT)) * jnp.exp2(exponent.astype(jnp.float32))
    return jnp.where(code < 0, -value, value)


def largest(value):
    return jnp.max(jnp.abs(value), axis=0, keepdims=True)


def conv_kernel(scale, lag_own, s_ref, left_ref, t_ref, out_ref, s_hi, s_lo, grads, cross, lag_sums):
    blocks, tok = 2 * s_ref.shape[0], left_ref.shape[1] // 2
    groups, rows, _ = grads.shape
    per = rows // blocks
    width = t_ref.shape[2]
    steps = width // tok
    used = min(steps, blocks)
    g = pl.program_id(0)

    @pl.when(g == 0)
    def _():
        s_hi[:, rows:, :] = jnp.zeros_like(s_hi[:, rows:, :])
        s_lo[:, rows:, :] = jnp.zeros_like(s_lo[:, rows:, :])
        for a in range(blocks):
            z, rest = divmod(a, blocks // 4)
            source, first = z // 2 * (blocks // 4) + rest, z % 2 * tok
            code, exponent = s_ref[source, first : first + tok, :], s_ref[source, 2 * tok : 2 * tok + 1, :]
            high, low = split(decoded(code, exponent).T[: groups * per])
            s_hi[:, a * per : (a + 1) * per, :] = high.reshape(groups, per, tok)
            s_lo[:, a * per : (a + 1) * per, :] = low.reshape(groups, per, tok)

    for d in range(0, used, 2):
        first, second = d * per, (d + 1) * per
        count = rows - first
        left = jnp.concatenate(
            [
                jnp.concatenate([ref[g, first : first + count, :], ref[g, second : second + count, :]], axis=1)
                for ref in (s_hi, s_lo)
            ],
            axis=0,
        )
        if d + 2 <= steps:
            right = t_ref[0, :, d * tok : (d + 2) * tok]
        else:
            right = jnp.concatenate([t_ref[0, :, d * tok :], jnp.zeros((2 * tok, tok), jnp.bfloat16)], axis=1)
        product = lax.dot_general(left, right, (((1,), (1,)), ((), ())), preferred_element_type=jnp.float32)
        term = product[:count, :tok] + (product[:count, tok:] + product[count:, :tok])
        if d == 0:
            grads[g] = term
        else:
            grads[g, :count, :] += term

    for d in range(0, used, 2):
        depth = min(rows, -(-(rows - d * per) // LANES) * LANES)
        high, low = [
            jnp.concatenate([ref[g, d * per : d * per + depth, :], ref[g, (d + 1) * per : (d + 1) * per + depth, :]], axis=1)
            for ref in (s_hi, s_lo)
        ]
        main = jnp.dot(left_ref[0, :, :depth], high, preferred_element_type=jnp.float32)
        rest = jnp.dot(left_ref[0, :tok, :depth], low, preferred_element_type=jnp.float32)
        stop = min(d + 2, steps)
        cross[:, d * tok : stop * tok] = (main[:tok] + (main[tok:] + rest))[:, : (stop - d) * tok]
    if used + used % 2 < steps:
        cross[:, (used + used % 2) * tok :] = jnp.zeros_like(cross[:, (used + used % 2) * tok :])
    skewed = pltpu.roll(cross[...], width - tok + 1, 1, stride=1, stride_axis=0)
    lag_sums[pl.ds(g, 1), :] = jnp.sum(skewed, axis=0, keepdims=True)[:, : width - tok] * scale

    @pl.when(g == groups - 1)
    def _():
        lags, lag_exponent = coded(lag_sums[...], largest(lag_sums[...]))
        held = out_ref.shape[1] - 8
        for a in range(blocks):
            out_ref[a, tok:held, :] = jnp.zeros_like(out_ref[a, tok:held, :])
            block = grads[:, a * per : (a + 1) * per, :].reshape(groups * per, tok).T
            code, exponent = coded(block, largest(block))
            if out_ref.shape[2] > groups * per:
                out_ref[a, :tok, :] = jnp.zeros_like(out_ref[a, :tok, :])
            out_ref[a, held:, :] = jnp.zeros_like(out_ref[a, held:, :])
            out_ref[a, :tok, : groups * per] = code
            out_ref[a, held : held + 1, : groups * per] = exponent
            own_lags = slice(a * lag_own, (a + 1) * lag_own)
            out_ref[a, tok : tok + groups, :lag_own] = lags[:, own_lags]
            out_ref[a, held + 1 : held + 2, :lag_own] = lag_exponent[:, own_lags]


def convolve(seq_blocks, input_blocks, moved, channels, lag_own, scale):
    blocks, tok, own = input_blocks.shape
    groups, _, width = moved.shape
    per = -(-channels // ROW_TILE) * ROW_TILE
    if groups * per != LANES or channels != per:
        wide = groups * per
        lanes = -(-wide // LANES) * LANES

        def widen(v):
            shape = v.shape[:-1]
            v = v.reshape(-1, groups, channels)
            v = jnp.pad(v, ((0, 0), (0, 0), (0, per - channels))).reshape(-1, wide)
            return jnp.pad(v, ((0, 0), (0, lanes - wide))).reshape(shape + (lanes,))

        seq_blocks, input_blocks = widen(seq_blocks), widen(input_blocks)
    rows = blocks * per
    left = stack_input(input_blocks, groups, per)
    extra = -(-(groups + 8) // ROW_TILE) * ROW_TILE
    out_lanes = max(groups * per, lag_own)
    return pl.pallas_call(
        functools.partial(conv_kernel, scale, lag_own),
        grid=(groups,),
        in_specs=[
            pl.BlockSpec(seq_blocks.shape, lambda g: (0, 0, 0)),
            pl.BlockSpec((1, 2 * tok, rows), lambda g: (g, 0, 0)),
            pl.BlockSpec((1, 2 * tok, width), lambda g: (g, 0, 0)),
        ],
        out_specs=pl.BlockSpec((blocks, tok + extra, out_lanes), lambda g: (0, 0, 0)),
        out_shape=jax.ShapeDtypeStruct((blocks, tok + extra, out_lanes), jnp.float32),
        scratch_shapes=[pltpu.VMEM((groups, 2 * rows, tok), jnp.bfloat16)] * 2
        + [
            pltpu.VMEM((groups, rows, tok), jnp.float32),
            pltpu.VMEM((tok, width), jnp.float32),
            pltpu.VMEM((groups, width - tok), jnp.float32),
        ],
        compiler_params=pltpu.CompilerParams(vmem_limit_bytes=48 * 1024 * 1024),
        cost_estimate=pl.CostEstimate(
            flops=groups * rows * tok * width * 14,
            bytes_accessed=12 * blocks * tok * LANES + 4 * groups * tok * width,
            transcendentals=0,
        ),
        name="convolve",
    )(seq_blocks, left, moved)


def nothing(*refs):
    del refs


def after(value, *earlier):
    return pl.pallas_call(
        nothing,
        in_specs=[ANY] * (1 + len(earlier)),
        out_specs=ANY,
        out_shape=jax.ShapeDtypeStruct(value.shape, value.dtype),
        input_output_aliases={0: 0},
        compiler_params=pltpu.CompilerParams(vmem_limit_bytes=1 * 1024 * 1024),
        cost_estimate=pl.CostEstimate(flops=0, bytes_accessed=0, transcendentals=0),
        name="after",
    )(value, *earlier)


class Place:
    def __init__(self):
        self.devices = lax.axis_size("ctx")
        self.ys = self.devices // 8
        assert self.devices == 8 * self.ys
        me = lax.axis_index("ctx")
        self.core, chip = lax.rem(me, 2), me // 2
        self.y, z = lax.rem(chip, self.ys), chip // self.ys
        self.p, self.h = lax.rem(z, 2), z // 2
        self.block = (self.h * self.ys + self.y) * 2 + self.core

    def index(self, h, p, y, core):
        return ((h * 2 + p) * self.ys + y) * 2 + core

    def all(self):
        return [(h, p, y, c) for h in range(2) for p in range(2) for y in range(self.ys) for c in range(2)]

    def swap_core(self, v):
        return lax.ppermute(v, "ctx", [(self.index(h, p, y, c), self.index(h, p, y, 1 - c)) for h, p, y, c in self.all()])

    def swap_pair(self, v):
        return lax.ppermute(v, "ctx", [(self.index(h, p, y, c), self.index(h, 1 - p, y, c)) for h, p, y, c in self.all()])

    def swap_half(self, v):
        return lax.ppermute(v, "ctx", [(self.index(h, p, y, c), self.index(1 - h, p, y, c)) for h, p, y, c in self.all()])

    def swap_half_and_pair(self, v):
        pairs = [(self.index(h, p, y, c), self.index(1 - h, 1 - p, y, c)) for h, p, y, c in self.all()]
        return lax.ppermute(v, "ctx", pairs)

    def along_y(self, v, shift):
        ys = self.ys
        return lax.ppermute(
            v, "ctx", [(self.index(h, p, y, c), self.index(h, p, (y + shift) % ys, c)) for h, p, y, c in self.all()]
        )

    def same_p(self):
        return [[self.index(h, p, y, c) for h in range(2) for y in range(self.ys) for c in range(2)] for p in range(2)]


def pick_kernel(features, slots, core_ref, *refs):
    parts, (mine_ref, theirs_ref) = refs[: 2 * slots], refs[-2:]
    tok, held = parts[0].shape
    first = core_ref[0] == 0
    for row in range(2):
        rows = slice(row * tok, (row + 1) * tok)
        for s in range(slots):
            part = parts[row * slots + s]
            for b in range(held // (2 * features)):
                even = part[:, 2 * b * features : (2 * b + 1) * features]
                odd = part[:, (2 * b + 1) * features : (2 * b + 2) * features]
                at = s * held // 2 + b * features
                mine_ref[rows, at : at + features] = jnp.where(first, even, odd)
                theirs_ref[rows, at : at + features] = jnp.where(first, odd, even)


def gather_cotangent(cotangent, features, place, earlier):
    tok, held = cotangent.shape
    parts = lax.axis_size("ch")
    far = place.swap_pair(cotangent)

    def along_ch(v):
        return [v] + [lax.ppermute(v, "ch", [(j, (j + s) % parts) for j in range(parts)]) for s in range(1, parts)]

    whole = jax.ShapeDtypeStruct((2 * tok, parts * held // 2), cotangent.dtype)
    mine, theirs = pl.pallas_call(
        functools.partial(pick_kernel, features, parts),
        in_specs=[SMEM] + [VMEM] * (2 * parts),
        out_specs=[VMEM] * 2,
        out_shape=[whole, whole],
        compiler_params=pltpu.CompilerParams(vmem_limit_bytes=10 * 1024 * 1024),
        cost_estimate=pl.CostEstimate(flops=0, bytes_accessed=8 * tok * held * parts, transcendentals=0),
        name="pick_features",
    )(place.core.reshape(1), *along_ch(cotangent), *along_ch(far))
    return mine, place.swap_core(after(theirs, *earlier))


def seq_kernel(p_ref, sum_ref, arrived_ref, gate_ref, far_gate_ref, *refs):
    out_ref, near_ref, far_ref = refs[-3:]
    p = p_ref[0]
    blocks, _, own = out_ref.shape
    tok = near_ref.shape[0]
    near_ref[...] = sum_ref[:tok, :] + arrived_ref[:tok, :]
    far_ref[...] = sum_ref[tok:, :] + arrived_ref[tok:, :]
    near = near_ref[...] * gate_ref[...]
    far = far_ref[...] * far_gate_ref[...]
    for b in range(blocks):
        here = slice(b * own, (b + 1) * own)
        most = jnp.maximum(largest(near[:, here]), largest(far[:, here]))
        for value, place in ((near, p), (far, 1 - p)):
            code, exponent = coded(value[:, here], most)
            out_ref[b, pl.ds(pl.multiple_of(place * tok, tok), tok), :] = code
        out_ref[b, 2 * tok :, :] = jnp.broadcast_to(exponent, (ROW_TILE, own))


def seq_blocks_of(total, arrived, gate_value, far_gate, place, *awaited):
    tok, channels = gate_value.shape
    blocks = place.devices // 2
    half = channels // 2
    own = half // blocks
    steps = max(1, min(4, half // LANES))
    width, count = half // steps, blocks // steps
    return pl.pallas_call(
        seq_kernel,
        grid_spec=pltpu.PrefetchScalarGridSpec(
            num_scalar_prefetch=1,
            grid=(steps,),
            in_specs=[
                pl.BlockSpec((2 * tok, width), lambda i, p: (0, i)),
                pl.BlockSpec((2 * tok, width), lambda i, p: (0, i)),
                pl.BlockSpec((tok, width), lambda i, p: (0, p[0] * steps + i)),
                pl.BlockSpec((tok, width), lambda i, p: (0, i)),
            ]
            + [ANY] * len(awaited),
            out_specs=[
                pl.BlockSpec((count, 2 * tok + ROW_TILE, own), lambda i, p: (i, 0, 0)),
                pl.BlockSpec((tok, width), lambda i, p: (0, i)),
                pl.BlockSpec((tok, width), lambda i, p: (0, i)),
            ],
        ),
        out_shape=[
            jax.ShapeDtypeStruct((blocks, 2 * tok + ROW_TILE, own), jnp.float32),
            jax.ShapeDtypeStruct((tok, half), jnp.float32),
            jax.ShapeDtypeStruct((tok, half), jnp.float32),
        ],
        compiler_params=pltpu.CompilerParams(vmem_limit_bytes=12 * 1024 * 1024),
        cost_estimate=pl.CostEstimate(
            flops=2 * tok * channels, bytes_accessed=24 * tok * channels, transcendentals=0
        ),
        name="seq_grad",
    )(place.p.reshape(1), total, arrived, gate_value, far_gate, *awaited)


def column_of(share, ctx, ch, ys, parts, features):
    other_h, other_p, shift = share
    chip = ctx // 2
    z, y = chip // ys, lax.rem(chip, ys)
    h, p = z // 2, lax.rem(z, 2)
    source = ((1 - h if other_h else h) * 2 + (1 - p if other_p else p)) * ys + lax.rem(y - shift + ys, ys)
    chips = 4 * ys // parts
    return (lax.rem(ch - source // chips + parts, parts) * chips + lax.rem(source, chips)) * features


def share_kernel(where, ys, parts, ctx_ref, ch_ref, mine_ref, theirs_ref, *refs):
    shares, before, (own_ref, other_ref) = refs[: len(where)], refs[len(where) : -2], refs[-2:]
    rows, features = mine_ref.shape[0], shares[0].shape[1]
    left = []
    for share in where:
        column = column_of(share, ctx_ref[0], ch_ref[0], ys, parts, features)
        at = pl.ds(pl.multiple_of(column, features), features)
        left.append(jnp.concatenate([mine_ref[:, at], theirs_ref[:, at]], axis=0))
    term = lax.dot_general(
        jnp.concatenate(left, axis=1),
        jnp.concatenate([share[...] for share in shares], axis=1),
        (((1,), (1,)), ((), ())),
        preferred_element_type=jnp.float32,
    )
    for i, ref in enumerate((own_ref, other_ref)):
        part = term[i * rows : (i + 1) * rows]
        ref[...] = part + before[i][...] if before else part


def add_shares(where, mine, theirs, shares, before, place):
    rows, (half, features) = mine.shape[0], shares[0].shape
    parts = lax.axis_size("ch")
    ctx, ch = lax.axis_index("ctx"), lax.axis_index("ch")
    if features % LANES:
        sums = list(before)
        for share, held in zip(where, shares):
            column = column_of(share, ctx, ch, place.ys, parts, features)
            terms = [
                lax.dot_general(
                    lax.dynamic_slice_in_dim(v, column, features, 1),
                    held,
                    (((1,), (1,)), ((), ())),
                    preferred_element_type=jnp.float32,
                )
                for v in (mine, theirs)
            ]
            sums = [a + b for a, b in zip(sums, terms)] if sums else terms
        return sums
    tile = min(256, half)
    whole = jax.ShapeDtypeStruct((rows, half), jnp.float32)
    tiles = pl.BlockSpec((rows, tile), lambda n: (0, n))
    return pl.pallas_call(
        functools.partial(share_kernel, where, place.ys, parts),
        grid=(half // tile,),
        in_specs=[SMEM] * 2
        + [pl.BlockSpec(mine.shape, lambda n: (0, 0))] * 2
        + [pl.BlockSpec((tile, features), lambda n: (n, 0))] * len(shares)
        + [tiles] * len(before),
        out_specs=[tiles] * 2,
        out_shape=[whole, whole],
        compiler_params=pltpu.CompilerParams(vmem_limit_bytes=GRANT),
        cost_estimate=pl.CostEstimate(
            flops=4 * rows * half * len(shares) * features,
            bytes_accessed=2 * (mine.size * 2 + half * len(shares) * features) + 16 * rows * half,
            transcendentals=0,
        ),
        name="add_shares",
    )(ctx.reshape(1), ch.reshape(1), mine, theirs, *shares, *before)


def project(cotangent, out_weight, place, waited, between):
    channels, features = out_weight.shape
    half = channels // 2
    near = lax.dynamic_slice_in_dim(out_weight, place.p * half, half, 0)
    given = lax.dynamic_slice_in_dim(out_weight, (1 - place.p) * half, half, 0)
    far = place.swap_half(near)
    paired = place.swap_pair(given)
    far_paired = place.swap_half_and_pair(after(given, far))

    def along_y(v):
        return [v] + [place.along_y(v, shift) for shift in range(1, place.ys)]

    held = [along_y(near)]
    held.append(along_y(after(paired, *held[0][1:])))
    held.append(along_y(far))
    held.append(along_y(after(far_paired, *held[1][1:], *held[2][1:])))
    made = between(held[2][-1])
    mine, theirs = gather_cotangent(cotangent, features, place, [*held[3][1:], waited, made])
    shares = [
        ((other // 2, other % 2, shift), held[other][shift]) for other in range(4) for shift in range(place.ys)
    ]
    sums = []
    for some in (shares,):
        sums = add_shares([at for at, _ in some], mine, theirs, [v for _, v in some], sums, place)
    own, other = sums
    return own, place.swap_core(other), made


def code_kernel(x_ref, *refs):
    out_ref = refs[-1]
    devices, rows, own = out_ref.shape
    tok = x_ref.shape[0]
    code, exponent = coded(x_ref[...], largest(x_ref[...]))
    quarter = devices // 4
    for i in range(devices):
        h, p, rest = i // (2 * quarter), i // quarter % 2, i % quarter
        block = (p * 2 + h) * quarter + rest
        out_ref[i, :tok, :] = code[:, block * own : (block + 1) * own]
        out_ref[i, tok:, :] = jnp.broadcast_to(exponent[:, block * own : (block + 1) * own], (rows - tok, own))


def code_blocks(value, devices, *awaited):
    tok, channels = value.shape
    return pl.pallas_call(
        code_kernel,
        in_specs=[VMEM] + [ANY] * len(awaited),
        out_specs=VMEM,
        out_shape=jax.ShapeDtypeStruct((devices, tok + ROW_TILE, channels // devices), jnp.float32),
        compiler_params=pltpu.CompilerParams(vmem_limit_bytes=8 * 1024 * 1024),
        cost_estimate=pl.CostEstimate(flops=4 * tok * channels, bytes_accessed=8 * tok * channels, transcendentals=0),
        name="code_input",
    )(value, *awaited)


def body(cotangent, out_weight, gate_value, conv_output, conv_input, filters):
    tok, channels = gate_value.shape
    all_groups, lags = filters.shape
    place = Place()
    devices = place.devices
    per_group = channels // all_groups
    own = channels // devices
    half = channels // 2
    groups = max(1, own // per_group)
    share = max(1, per_group // own)
    lag_own = lags // devices

    def exchange(blocks, groups=None):
        return lax.all_to_all(blocks, "ctx", 0, 0, tiled=True, axis_index_groups=groups)

    def reorder(blocks):
        return blocks.reshape((2, 2, devices // 4) + blocks.shape[1:]).swapaxes(0, 1).reshape(blocks.shape)

    far_gate = place.swap_pair(lax.dynamic_slice_in_dim(gate_value, (1 - place.p) * half, half, 1))
    total, arrived, code = project(
        cotangent, out_weight, place, far_gate, lambda earlier: code_blocks(conv_input, devices, earlier)
    )
    code = exchange(code.astype(jnp.float16))
    input_blocks = decoded(code[:, :tok], code[:, tok : tok + 1])
    first_group = (place.p * half + place.block * own) // per_group
    moved = toeplitz(lax.dynamic_slice_in_dim(filters, first_group, groups, 0), tok)

    seq_code, near, far = seq_blocks_of(total, arrived, gate_value, far_gate, place)
    seq_code = exchange(seq_code.astype(jnp.float16), place.same_p())
    seq_blocks = seq_code.astype(jnp.float32)
    far = place.swap_pair(far)
    left = jnp.where(place.p == 0, near, far)
    right = jnp.where(place.p == 0, far, near)
    gate_grad = jnp.concatenate([left, right], axis=1) * conv_output

    scale = 1.0 / math.sqrt(per_group * tok * devices)
    result = convolve(seq_blocks, input_blocks, moved, min(own, per_group), lag_own, scale)
    back = exchange(result[:, :, : max(own, lag_own)].astype(jnp.float16))
    held = back.shape[1] - 8
    input_grad = reorder(decoded(back[:, :tok, :own], back[:, held : held + 1, :own]))
    input_grad = input_grad.transpose(1, 0, 2).reshape(tok, channels)
    filter_grad = reorder(decoded(back[:, tok : tok + groups, :lag_own], back[:, held + 1 : held + 2, :lag_own]))
    filter_grad = filter_grad.reshape(all_groups, share, lag_own).sum(axis=1)
    return (input_grad, gate_grad, filter_grad)


def solution(mesh):
    return jax.shard_map(
        body,
        mesh=mesh,
        in_specs=(
            P("ctx", "ch"),
            P("ch", "ctx"),
            P("ctx", "ch"),
            P("ctx", "ch"),
            P("ctx", "ch"),
            P("ch", None),
        ),
        out_specs=(P("ctx", "ch"), P("ctx", "ch"), P("ch", "ctx")),
        check_vma=False,
    )
```

```python
import functools
import math

import jax
import jax.numpy as jnp
from jax import lax
from jax.experimental import pallas as pl
from jax.experimental.pallas import tpu as pltpu
from jax.sharding import PartitionSpec as P

LANES = 128
ROW_TILE = 16
GRANT = 60 * 1024 * 1024
CODE_UNIT = 8192.0
SMALLEST = 1e-30
VMEM = pl.BlockSpec(memory_space=pltpu.VMEM)
SMEM = pl.BlockSpec(memory_space=pltpu.SMEM)
ANY = pl.BlockSpec(memory_space=pl.ANY)


def split(value):
    high = value.astype(jnp.bfloat16)
    return high, (value - high.astype(jnp.float32)).astype(jnp.bfloat16)


def toeplitz_kernel(filter_ref, out_ref):
    tok = out_ref.shape[1] // 2
    rows = jnp.broadcast_to(filter_ref[0], (tok, filter_ref.shape[2]))
    high, low = split(pltpu.roll(rows, 0, 1, stride=1, stride_axis=0))
    out_ref[0, :tok, :] = high
    out_ref[0, tok:, :] = low


def toeplitz(filters, tok):
    groups, lags = filters.shape
    width = lags + tok
    padded = jnp.pad(filters, ((0, 0), (0, tok)))[:, None, :]
    return pl.pallas_call(
        toeplitz_kernel,
        grid=(groups,),
        in_specs=[pl.BlockSpec((1, 1, width), lambda g: (g, 0, 0))],
        out_specs=pl.BlockSpec((1, 2 * tok, width), lambda g: (g, 0, 0)),
        out_shape=jax.ShapeDtypeStruct((groups, 2 * tok, width), jnp.bfloat16),
        compiler_params=pltpu.CompilerParams(vmem_limit_bytes=8 * 1024 * 1024),
        cost_estimate=pl.CostEstimate(
            flops=groups * tok * width * 4, bytes_accessed=groups * width * (4 + 4 * tok), transcendentals=0
        ),
        name="toeplitz",
    )(padded)


def stack_kernel(x_ref, left_ref, x_hi, x_lo):
    blocks, tok, _ = x_ref.shape
    groups, rows, _ = x_hi.shape
    per = rows // blocks

    @pl.loop(0, blocks)
    def _(a):
        at = pl.ds(pl.multiple_of(a * per, per), per)
        high, low = split(x_ref[a].T[: groups * per])
        x_hi[:, at, :] = high.reshape(groups, per, tok)
        x_lo[:, at, :] = low.reshape(groups, per, tok)

    last = lax.broadcasted_iota(jnp.int32, (tok, tok), 0) + lax.broadcasted_iota(jnp.int32, (tok, tok), 1)
    turn = jnp.where(last == tok - 1, 1.0, 0.0).astype(jnp.bfloat16)

    @pl.loop(0, groups)
    def _(g):
        for half, ref in ((0, x_hi), (1, x_lo)):
            turned = lax.dot_general(turn, ref[g], (((1,), (1,)), ((), ())), preferred_element_type=jnp.float32)
            left_ref[g, half * tok : (half + 1) * tok, :] = turned.astype(jnp.bfloat16)


def stack_input(input_blocks, groups, per):
    blocks, tok, lanes = input_blocks.shape
    rows = blocks * per
    return pl.pallas_call(
        stack_kernel,
        in_specs=[VMEM],
        out_specs=VMEM,
        out_shape=jax.ShapeDtypeStruct((groups, 2 * tok, rows), jnp.bfloat16),
        scratch_shapes=[pltpu.VMEM((groups, rows, tok), jnp.bfloat16)] * 2,
        compiler_params=pltpu.CompilerParams(vmem_limit_bytes=12 * 1024 * 1024),
        cost_estimate=pl.CostEstimate(
            flops=blocks * tok * lanes * 8, bytes_accessed=blocks * tok * lanes * 8, transcendentals=0
        ),
        name="stack_input",
    )(input_blocks)


def coded(value, most):
    exponent = jnp.floor(jnp.log2(jnp.maximum(most, SMALLEST)))
    v = value * jnp.exp2(-exponent)
    return v * jnp.abs(v) * CODE_UNIT, exponent


def decoded(code, exponent):
    code = code.astype(jnp.float32)
    value = jnp.sqrt(jnp.abs(code) * (1.0 / CODE_UNIT)) * jnp.exp2(exponent.astype(jnp.float32))
    return jnp.where(code < 0, -value, value)


def largest(value):
    return jnp.max(jnp.abs(value), axis=0, keepdims=True)


def conv_kernel(scale, lag_own, s_ref, left_ref, t_ref, out_ref, s_hi, s_lo, grads, cross, lag_sums):
    blocks, tok = 2 * s_ref.shape[0], left_ref.shape[1] // 2
    groups, rows, _ = grads.shape
    per = rows // blocks
    width = t_ref.shape[2]
    steps = width // tok
    used = min(steps, blocks)
    g = pl.program_id(0)

    @pl.when(g == 0)
    def _():
        s_hi[:, rows:, :] = jnp.zeros_like(s_hi[:, rows:, :])
        s_lo[:, rows:, :] = jnp.zeros_like(s_lo[:, rows:, :])
        for a in range(blocks):
            z, rest = divmod(a, blocks // 4)
            source, first = z // 2 * (blocks // 4) + rest, z % 2 * tok
            code, exponent = s_ref[source, first : first + tok, :], s_ref[source, 2 * tok : 2 * tok + 1, :]
            high, low = split(decoded(code, exponent).T[: groups * per])
            s_hi[:, a * per : (a + 1) * per, :] = high.reshape(groups, per, tok)
            s_lo[:, a * per : (a + 1) * per, :] = low.reshape(groups, per, tok)

    for d in range(0, used, 2):
        first, second = d * per, (d + 1) * per
        count = rows - first
        left = jnp.concatenate(
            [
                jnp.concatenate([ref[g, first : first + count, :], ref[g, second : second + count, :]], axis=1)
                for ref in (s_hi, s_lo)
            ],
            axis=0,
        )
        if d + 2 <= steps:
            right = t_ref[0, :, d * tok : (d + 2) * tok]
        else:
            right = jnp.concatenate([t_ref[0, :, d * tok :], jnp.zeros((2 * tok, tok), jnp.bfloat16)], axis=1)
        product = lax.dot_general(left, right, (((1,), (1,)), ((), ())), preferred_element_type=jnp.float32)
        term = product[:count, :tok] + (product[:count, tok:] + product[count:, :tok])
        if d == 0:
            grads[g] = term
        else:
            grads[g, :count, :] += term

    for d in range(0, used, 2):
        depth = min(rows, -(-(rows - d * per) // LANES) * LANES)
        high, low = [
            jnp.concatenate([ref[g, d * per : d * per + depth, :], ref[g, (d + 1) * per : (d + 1) * per + depth, :]], axis=1)
            for ref in (s_hi, s_lo)
        ]
        main = jnp.dot(left_ref[0, :, :depth], high, preferred_element_type=jnp.float32)
        rest = jnp.dot(left_ref[0, :tok, :depth], low, preferred_element_type=jnp.float32)
        stop = min(d + 2, steps)
        cross[:, d * tok : stop * tok] = (main[:tok] + (main[tok:] + rest))[:, : (stop - d) * tok]
    if used + used % 2 < steps:
        cross[:, (used + used % 2) * tok :] = jnp.zeros_like(cross[:, (used + used % 2) * tok :])
    skewed = pltpu.roll(cross[...], width - tok + 1, 1, stride=1, stride_axis=0)
    lag_sums[pl.ds(g, 1), :] = jnp.sum(skewed, axis=0, keepdims=True)[:, : width - tok] * scale

    @pl.when(g == groups - 1)
    def _():
        lags, lag_exponent = coded(lag_sums[...], largest(lag_sums[...]))
        held = out_ref.shape[1] - 8
        for a in range(blocks):
            out_ref[a, tok:held, :] = jnp.zeros_like(out_ref[a, tok:held, :])
            block = grads[:, a * per : (a + 1) * per, :].reshape(groups * per, tok).T
            code, exponent = coded(block, largest(block))
            if out_ref.shape[2] > groups * per:
                out_ref[a, :tok, :] = jnp.zeros_like(out_ref[a, :tok, :])
            out_ref[a, held:, :] = jnp.zeros_like(out_ref[a, held:, :])
            out_ref[a, :tok, : groups * per] = code
            out_ref[a, held : held + 1, : groups * per] = exponent
            own_lags = slice(a * lag_own, (a + 1) * lag_own)
            out_ref[a, tok : tok + groups, :lag_own] = lags[:, own_lags]
            out_ref[a, held + 1 : held + 2, :lag_own] = lag_exponent[:, own_lags]


def convolve(seq_blocks, input_blocks, moved, channels, lag_own, scale):
    blocks, tok, own = input_blocks.shape
    groups, _, width = moved.shape
    per = -(-channels // ROW_TILE) * ROW_TILE
    if groups * per != LANES or channels != per:
        wide = groups * per
        lanes = -(-wide // LANES) * LANES

        def widen(v):
            shape = v.shape[:-1]
            v = v.reshape(-1, groups, channels)
            v = jnp.pad(v, ((0, 0), (0, 0), (0, per - channels))).reshape(-1, wide)
            return jnp.pad(v, ((0, 0), (0, lanes - wide))).reshape(shape + (lanes,))

        seq_blocks, input_blocks = widen(seq_blocks), widen(input_blocks)
    rows = blocks * per
    left = stack_input(input_blocks, groups, per)
    extra = -(-(groups + 8) // ROW_TILE) * ROW_TILE
    out_lanes = max(groups * per, lag_own)
    return pl.pallas_call(
        functools.partial(conv_kernel, scale, lag_own),
        grid=(groups,),
        in_specs=[
            pl.BlockSpec(seq_blocks.shape, lambda g: (0, 0, 0)),
            pl.BlockSpec((1, 2 * tok, rows), lambda g: (g, 0, 0)),
            pl.BlockSpec((1, 2 * tok, width), lambda g: (g, 0, 0)),
        ],
        out_specs=pl.BlockSpec((blocks, tok + extra, out_lanes), lambda g: (0, 0, 0)),
        out_shape=jax.ShapeDtypeStruct((blocks, tok + extra, out_lanes), jnp.float32),
        scratch_shapes=[pltpu.VMEM((groups, 2 * rows, tok), jnp.bfloat16)] * 2
        + [
            pltpu.VMEM((groups, rows, tok), jnp.float32),
            pltpu.VMEM((tok, width), jnp.float32),
            pltpu.VMEM((groups, width - tok), jnp.float32),
        ],
        compiler_params=pltpu.CompilerParams(vmem_limit_bytes=48 * 1024 * 1024),
        cost_estimate=pl.CostEstimate(
            flops=groups * rows * tok * width * 14,
            bytes_accessed=12 * blocks * tok * LANES + 4 * groups * tok * width,
            transcendentals=0,
        ),
        name="convolve",
    )(seq_blocks, left, moved)


def nothing(*refs):
    del refs


def after(value, *earlier):
    return pl.pallas_call(
        nothing,
        in_specs=[ANY] * (1 + len(earlier)),
        out_specs=ANY,
        out_shape=jax.ShapeDtypeStruct(value.shape, value.dtype),
        input_output_aliases={0: 0},
        compiler_params=pltpu.CompilerParams(vmem_limit_bytes=1 * 1024 * 1024),
        cost_estimate=pl.CostEstimate(flops=0, bytes_accessed=0, transcendentals=0),
        name="after",
    )(value, *earlier)


class Place:
    def __init__(self):
        self.devices = lax.axis_size("ctx")
        self.ys = self.devices // 8
        assert self.devices == 8 * self.ys
        me = lax.axis_index("ctx")
        self.core, chip = lax.rem(me, 2), me // 2
        self.y, z = lax.rem(chip, self.ys), chip // self.ys
        self.p, self.h = lax.rem(z, 2), z // 2
        self.block = (self.h * self.ys + self.y) * 2 + self.core

    def index(self, h, p, y, core):
        return ((h * 2 + p) * self.ys + y) * 2 + core

    def all(self):
        return [(h, p, y, c) for h in range(2) for p in range(2) for y in range(self.ys) for c in range(2)]

    def swap_core(self, v):
        return lax.ppermute(v, "ctx", [(self.index(h, p, y, c), self.index(h, p, y, 1 - c)) for h, p, y, c in self.all()])

    def swap_pair(self, v):
        return lax.ppermute(v, "ctx", [(self.index(h, p, y, c), self.index(h, 1 - p, y, c)) for h, p, y, c in self.all()])

    def swap_half(self, v):
        return lax.ppermute(v, "ctx", [(self.index(h, p, y, c), self.index(1 - h, p, y, c)) for h, p, y, c in self.all()])

    def swap_half_and_pair(self, v):
        pairs = [(self.index(h, p, y, c), self.index(1 - h, 1 - p, y, c)) for h, p, y, c in self.all()]
        return lax.ppermute(v, "ctx", pairs)

    def along_y(self, v, shift):
        ys = self.ys
        return lax.ppermute(
            v, "ctx", [(self.index(h, p, y, c), self.index(h, p, (y + shift) % ys, c)) for h, p, y, c in self.all()]
        )

    def same_p(self):
        return [[self.index(h, p, y, c) for h in range(2) for y in range(self.ys) for c in range(2)] for p in range(2)]


def pick_kernel(features, slots, core_ref, *refs):
    parts, (mine_ref, theirs_ref) = refs[: 2 * slots], refs[-2:]
    tok, held = parts[0].shape
    first = core_ref[0] == 0
    for row in range(2):
        rows = slice(row * tok, (row + 1) * tok)
        for s in range(slots):
            part = parts[row * slots + s]
            for b in range(held // (2 * features)):
                even = part[:, 2 * b * features : (2 * b + 1) * features]
                odd = part[:, (2 * b + 1) * features : (2 * b + 2) * features]
                at = s * held // 2 + b * features
                mine_ref[rows, at : at + features] = jnp.where(first, even, odd)
                theirs_ref[rows, at : at + features] = jnp.where(first, odd, even)


def gather_cotangent(cotangent, features, place, earlier):
    tok, held = cotangent.shape
    parts = lax.axis_size("ch")
    far = place.swap_pair(cotangent)

    def along_ch(v):
        return [v] + [lax.ppermute(v, "ch", [(j, (j + s) % parts) for j in range(parts)]) for s in range(1, parts)]

    whole = jax.ShapeDtypeStruct((2 * tok, parts * held // 2), cotangent.dtype)
    mine, theirs = pl.pallas_call(
        functools.partial(pick_kernel, features, parts),
        in_specs=[SMEM] + [VMEM] * (2 * parts),
        out_specs=[VMEM] * 2,
        out_shape=[whole, whole],
        compiler_params=pltpu.CompilerParams(vmem_limit_bytes=10 * 1024 * 1024),
        cost_estimate=pl.CostEstimate(flops=0, bytes_accessed=8 * tok * held * parts, transcendentals=0),
        name="pick_features",
    )(place.core.reshape(1), *along_ch(cotangent), *along_ch(far))
    return mine, place.swap_core(after(theirs, *earlier))


def seq_kernel(p_ref, sum_ref, arrived_ref, gate_ref, far_gate_ref, *refs):
    out_ref, near_ref, far_ref = refs[-3:]
    p = p_ref[0]
    blocks, _, own = out_ref.shape
    tok = near_ref.shape[0]
    near_ref[...] = sum_ref[:tok, :] + arrived_ref[:tok, :]
    far_ref[...] = sum_ref[tok:, :] + arrived_ref[tok:, :]
    near = near_ref[...] * gate_ref[...]
    far = far_ref[...] * far_gate_ref[...]
    for b in range(blocks):
        here = slice(b * own, (b + 1) * own)
        most = jnp.maximum(largest(near[:, here]), largest(far[:, here]))
        for value, place in ((near, p), (far, 1 - p)):
            code, exponent = coded(value[:, here], most)
            out_ref[b, pl.ds(pl.multiple_of(place * tok, tok), tok), :] = code
        out_ref[b, 2 * tok :, :] = jnp.broadcast_to(exponent, (ROW_TILE, own))


def seq_blocks_of(total, arrived, gate_value, far_gate, place, *awaited):
    tok, channels = gate_value.shape
    blocks = place.devices // 2
    half = channels // 2
    own = half // blocks
    steps = max(1, min(4, half // LANES))
    width, count = half // steps, blocks // steps
    return pl.pallas_call(
        seq_kernel,
        grid_spec=pltpu.PrefetchScalarGridSpec(
            num_scalar_prefetch=1,
            grid=(steps,),
            in_specs=[
                pl.BlockSpec((2 * tok, width), lambda i, p: (0, i)),
                pl.BlockSpec((2 * tok, width), lambda i, p: (0, i)),
                pl.BlockSpec((tok, width), lambda i, p: (0, p[0] * steps + i)),
                pl.BlockSpec((tok, width), lambda i, p: (0, i)),
            ]
            + [ANY] * len(awaited),
            out_specs=[
                pl.BlockSpec((count, 2 * tok + ROW_TILE, own), lambda i, p: (i, 0, 0)),
                pl.BlockSpec((tok, width), lambda i, p: (0, i)),
                pl.BlockSpec((tok, width), lambda i, p: (0, i)),
            ],
        ),
        out_shape=[
            jax.ShapeDtypeStruct((blocks, 2 * tok + ROW_TILE, own), jnp.float32),
            pltpu.HBM((tok, half), jnp.float32),
            pltpu.HBM((tok, half), jnp.float32),
        ],
        compiler_params=pltpu.CompilerParams(vmem_limit_bytes=12 * 1024 * 1024),
        cost_estimate=pl.CostEstimate(
            flops=2 * tok * channels, bytes_accessed=24 * tok * channels, transcendentals=0
        ),
        name="seq_grad",
    )(place.p.reshape(1), total, arrived, gate_value, far_gate, *awaited)


def column_of(share, ctx, ch, ys, parts, features):
    other_h, other_p, shift = share
    chip = ctx // 2
    z, y = chip // ys, lax.rem(chip, ys)
    h, p = z // 2, lax.rem(z, 2)
    source = ((1 - h if other_h else h) * 2 + (1 - p if other_p else p)) * ys + lax.rem(y - shift + ys, ys)
    chips = 4 * ys // parts
    return (lax.rem(ch - source // chips + parts, parts) * chips + lax.rem(source, chips)) * features


def share_kernel(where, ys, parts, ctx_ref, ch_ref, mine_ref, theirs_ref, *refs):
    shares, before, (own_ref, other_ref) = refs[: len(where)], refs[len(where) : -2], refs[-2:]
    rows, features = mine_ref.shape[0], shares[0].shape[1]
    left = []
    for share in where:
        column = column_of(share, ctx_ref[0], ch_ref[0], ys, parts, features)
        at = pl.ds(pl.multiple_of(column, features), features)
        left.append(jnp.concatenate([mine_ref[:, at], theirs_ref[:, at]], axis=0))
    term = lax.dot_general(
        jnp.concatenate(left, axis=1),
        jnp.concatenate([share[...] for share in shares], axis=1),
        (((1,), (1,)), ((), ())),
        preferred_element_type=jnp.float32,
    )
    for i, ref in enumerate((own_ref, other_ref)):
        part = term[i * rows : (i + 1) * rows]
        ref[...] = part + before[i][...] if before else part


def add_shares(where, mine, theirs, shares, before, place):
    rows, (half, features) = mine.shape[0], shares[0].shape
    parts = lax.axis_size("ch")
    ctx, ch = lax.axis_index("ctx"), lax.axis_index("ch")
    if features % LANES:
        sums = list(before)
        for share, held in zip(where, shares):
            column = column_of(share, ctx, ch, place.ys, parts, features)
            terms = [
                lax.dot_general(
                    lax.dynamic_slice_in_dim(v, column, features, 1),
                    held,
                    (((1,), (1,)), ((), ())),
                    preferred_element_type=jnp.float32,
                )
                for v in (mine, theirs)
            ]
            sums = [a + b for a, b in zip(sums, terms)] if sums else terms
        return sums
    tile = min(512, half)
    whole = jax.ShapeDtypeStruct((rows, half), jnp.float32)
    tiles = pl.BlockSpec((rows, tile), lambda n: (0, n))
    return pl.pallas_call(
        functools.partial(share_kernel, where, place.ys, parts),
        grid=(half // tile,),
        in_specs=[SMEM] * 2
        + [pl.BlockSpec(mine.shape, lambda n: (0, 0))] * 2
        + [pl.BlockSpec((tile, features), lambda n: (n, 0))] * len(shares)
        + [tiles] * len(before),
        out_specs=[tiles] * 2,
        out_shape=[whole, whole],
        compiler_params=pltpu.CompilerParams(vmem_limit_bytes=GRANT),
        cost_estimate=pl.CostEstimate(
            flops=4 * rows * half * len(shares) * features,
            bytes_accessed=2 * (mine.size * 2 + half * len(shares) * features) + 16 * rows * half,
            transcendentals=0,
        ),
        name="add_shares",
    )(ctx.reshape(1), ch.reshape(1), mine, theirs, *shares, *before)


def project(cotangent, out_weight, place, waited, between):
    channels, features = out_weight.shape
    half = channels // 2
    near = lax.dynamic_slice_in_dim(out_weight, place.p * half, half, 0)
    given = lax.dynamic_slice_in_dim(out_weight, (1 - place.p) * half, half, 0)
    far = place.swap_half(near)
    paired = place.swap_pair(given)
    far_paired = place.swap_half_and_pair(after(given, far))

    def along_y(v):
        return [v] + [place.along_y(v, shift) for shift in range(1, place.ys)]

    held = [along_y(near)]
    held.append(along_y(after(paired, *held[0][1:])))
    held.append(along_y(far))
    held.append(along_y(after(far_paired, *held[1][1:], *held[2][1:])))
    made, sign = between(held[2][-1])
    mine, theirs = gather_cotangent(cotangent, features, place, [*held[3][1:], waited, sign])
    shares = [
        ((other // 2, other % 2, shift), held[other][shift]) for other in range(4) for shift in range(place.ys)
    ]
    sums = []
    for some in (shares,):
        sums = add_shares([at for at, _ in some], mine, theirs, [v for _, v in some], sums, place)
    own, other = sums
    return own, place.swap_core(other), made


def code_kernel(x_ref, *refs):
    out_ref = refs[-1]
    devices, rows, own = out_ref.shape
    tok = x_ref.shape[0]
    code, exponent = coded(x_ref[...], largest(x_ref[...]))
    quarter = devices // 4
    for i in range(devices):
        h, p, rest = i // (2 * quarter), i // quarter % 2, i % quarter
        block = (p * 2 + h) * quarter + rest
        out_ref[i, :tok, :] = code[:, block * own : (block + 1) * own]
        out_ref[i, tok:, :] = jnp.broadcast_to(exponent[:, block * own : (block + 1) * own], (rows - tok, own))


def code_blocks(value, devices, *awaited):
    tok, channels = value.shape
    return pl.pallas_call(
        code_kernel,
        in_specs=[VMEM] + [ANY] * len(awaited),
        out_specs=VMEM,
        out_shape=jax.ShapeDtypeStruct((devices, tok + ROW_TILE, channels // devices), jnp.float32),
        compiler_params=pltpu.CompilerParams(vmem_limit_bytes=8 * 1024 * 1024),
        cost_estimate=pl.CostEstimate(flops=4 * tok * channels, bytes_accessed=8 * tok * channels, transcendentals=0),
        name="code_input",
    )(value, *awaited)


def body(cotangent, out_weight, gate_value, conv_output, conv_input, filters):
    tok, channels = gate_value.shape
    all_groups, lags = filters.shape
    place = Place()
    devices = place.devices
    per_group = channels // all_groups
    own = channels // devices
    half = channels // 2
    groups = max(1, own // per_group)
    share = max(1, per_group // own)
    lag_own = lags // devices

    def exchange(blocks, groups=None):
        return lax.all_to_all(blocks, "ctx", 0, 0, tiled=True, axis_index_groups=groups)

    def reorder(blocks):
        return blocks.reshape((2, 2, devices // 4) + blocks.shape[1:]).swapaxes(0, 1).reshape(blocks.shape)

    far_gate = place.swap_pair(lax.dynamic_slice_in_dim(gate_value, (1 - place.p) * half, half, 1))

    def code_input(earlier):
        code = lax.optimization_barrier(code_blocks(conv_input, devices, earlier).astype(jnp.float16))
        return code, code[0, :8].astype(jnp.float32)

    total, arrived, code = project(cotangent, out_weight, place, far_gate, code_input)
    code = exchange(code)
    input_blocks = decoded(code[:, :tok], code[:, tok : tok + 1])
    first_group = (place.p * half + place.block * own) // per_group
    moved = toeplitz(lax.dynamic_slice_in_dim(filters, first_group, groups, 0), tok)

    seq_code, near, far = seq_blocks_of(total, arrived, gate_value, far_gate, place)
    seq_code = exchange(seq_code.astype(jnp.float16), place.same_p())
    seq_blocks = seq_code.astype(jnp.float32)
    far = place.swap_pair(far)
    left = jnp.where(place.p == 0, near, far)
    right = jnp.where(place.p == 0, far, near)
    gate_grad = jnp.concatenate([left, right], axis=1) * conv_output

    scale = 1.0 / math.sqrt(per_group * tok * devices)
    result = convolve(seq_blocks, input_blocks, moved, min(own, per_group), lag_own, scale)
    back = exchange(result[:, :, : max(own, lag_own)].astype(jnp.float16))
    held = back.shape[1] - 8
    input_grad = reorder(decoded(back[:, :tok, :own], back[:, held : held + 1, :own]))
    input_grad = input_grad.transpose(1, 0, 2).reshape(tok, channels)
    filter_grad = reorder(decoded(back[:, tok : tok + groups, :lag_own], back[:, held + 1 : held + 2, :lag_own]))
    filter_grad = filter_grad.reshape(all_groups, share, lag_own).sum(axis=1)
    return (input_grad, gate_grad, filter_grad)


def solution(mesh):
    return jax.shard_map(
        body,
        mesh=mesh,
        in_specs=(
            P("ctx", "ch"),
            P("ch", "ctx"),
            P("ctx", "ch"),
            P("ctx", "ch"),
            P("ctx", "ch"),
            P("ch", None),
        ),
        out_specs=(P("ctx", "ch"), P("ctx", "ch"), P("ch", "ctx")),
        check_vma=False,
    )
```

```python
import functools
import math

import jax
import jax.numpy as jnp
from jax import lax
from jax.experimental import pallas as pl
from jax.experimental.pallas import tpu as pltpu
from jax.sharding import PartitionSpec as P

LANES = 128
ROW_TILE = 16
GRANT = 60 * 1024 * 1024
CODE_UNIT = 8192.0
SMALLEST = 1e-30
VMEM = pl.BlockSpec(memory_space=pltpu.VMEM)
SMEM = pl.BlockSpec(memory_space=pltpu.SMEM)
ANY = pl.BlockSpec(memory_space=pl.ANY)


def split(value):
    high = value.astype(jnp.bfloat16)
    return high, (value - high.astype(jnp.float32)).astype(jnp.bfloat16)


def toeplitz_kernel(filter_ref, out_ref):
    tok = out_ref.shape[1] // 2
    rows = jnp.broadcast_to(filter_ref[0], (tok, filter_ref.shape[2]))
    high, low = split(pltpu.roll(rows, 0, 1, stride=1, stride_axis=0))
    out_ref[0, :tok, :] = high
    out_ref[0, tok:, :] = low


def toeplitz(filters, tok):
    groups, lags = filters.shape
    width = lags + tok
    padded = jnp.pad(filters, ((0, 0), (0, tok)))[:, None, :]
    return pl.pallas_call(
        toeplitz_kernel,
        grid=(groups,),
        in_specs=[pl.BlockSpec((1, 1, width), lambda g: (g, 0, 0))],
        out_specs=pl.BlockSpec((1, 2 * tok, width), lambda g: (g, 0, 0)),
        out_shape=jax.ShapeDtypeStruct((groups, 2 * tok, width), jnp.bfloat16),
        compiler_params=pltpu.CompilerParams(vmem_limit_bytes=8 * 1024 * 1024),
        cost_estimate=pl.CostEstimate(
            flops=groups * tok * width * 4, bytes_accessed=groups * width * (4 + 4 * tok), transcendentals=0
        ),
        name="toeplitz",
    )(padded)


def stack_kernel(x_ref, left_ref, x_hi, x_lo):
    blocks, tok, _ = x_ref.shape
    groups, rows, _ = x_hi.shape
    per = rows // blocks

    @pl.loop(0, blocks)
    def _(a):
        at = pl.ds(pl.multiple_of(a * per, per), per)
        high, low = split(x_ref[a].T[: groups * per])
        x_hi[:, at, :] = high.reshape(groups, per, tok)
        x_lo[:, at, :] = low.reshape(groups, per, tok)

    last = lax.broadcasted_iota(jnp.int32, (tok, tok), 0) + lax.broadcasted_iota(jnp.int32, (tok, tok), 1)
    turn = jnp.where(last == tok - 1, 1.0, 0.0).astype(jnp.bfloat16)

    @pl.loop(0, groups)
    def _(g):
        for half, ref in ((0, x_hi), (1, x_lo)):
            turned = lax.dot_general(turn, ref[g], (((1,), (1,)), ((), ())), preferred_element_type=jnp.float32)
            left_ref[g, half * tok : (half + 1) * tok, :] = turned.astype(jnp.bfloat16)


def stack_input(input_blocks, groups, per):
    blocks, tok, lanes = input_blocks.shape
    rows = blocks * per
    return pl.pallas_call(
        stack_kernel,
        in_specs=[VMEM],
        out_specs=VMEM,
        out_shape=jax.ShapeDtypeStruct((groups, 2 * tok, rows), jnp.bfloat16),
        scratch_shapes=[pltpu.VMEM((groups, rows, tok), jnp.bfloat16)] * 2,
        compiler_params=pltpu.CompilerParams(vmem_limit_bytes=12 * 1024 * 1024),
        cost_estimate=pl.CostEstimate(
            flops=blocks * tok * lanes * 8, bytes_accessed=blocks * tok * lanes * 8, transcendentals=0
        ),
        name="stack_input",
    )(input_blocks)


def coded(value, most):
    exponent = jnp.floor(jnp.log2(jnp.maximum(most, SMALLEST)))
    v = value * jnp.exp2(-exponent)
    return v * jnp.abs(v) * CODE_UNIT, exponent


def decoded(code, exponent):
    code = code.astype(jnp.float32)
    scale = jnp.exp2(exponent.astype(jnp.float32)) * (CODE_UNIT**-0.5)
    return code * lax.rsqrt(jnp.maximum(jnp.abs(code), SMALLEST)) * scale


def largest(value):
    return jnp.max(jnp.abs(value), axis=0, keepdims=True)


def conv_kernel(scale, lag_own, s_ref, left_ref, t_ref, out_ref, s_hi, s_lo, grads, cross, lag_sums):
    blocks, tok = 2 * s_ref.shape[0], left_ref.shape[1] // 2
    groups, rows, _ = grads.shape
    per = rows // blocks
    width = t_ref.shape[2]
    steps = width // tok
    used = min(steps, blocks)
    g = pl.program_id(0)

    @pl.when(g == 0)
    def _():
        s_hi[:, rows:, :] = jnp.zeros_like(s_hi[:, rows:, :])
        s_lo[:, rows:, :] = jnp.zeros_like(s_lo[:, rows:, :])
        for a in range(blocks):
            z, rest = divmod(a, blocks // 4)
            source, first = z // 2 * (blocks // 4) + rest, z % 2 * tok
            code, exponent = s_ref[source, first : first + tok, :], s_ref[source, 2 * tok : 2 * tok + 1, :]
            high, low = split(decoded(code, exponent).T[: groups * per])
            s_hi[:, a * per : (a + 1) * per, :] = high.reshape(groups, per, tok)
            s_lo[:, a * per : (a + 1) * per, :] = low.reshape(groups, per, tok)

    for d in range(0, used, 2):
        first, second = d * per, (d + 1) * per
        count = rows - first
        left = jnp.concatenate(
            [
                jnp.concatenate([ref[g, first : first + count, :], ref[g, second : second + count, :]], axis=1)
                for ref in (s_hi, s_lo)
            ],
            axis=0,
        )
        if d + 2 <= steps:
            right = t_ref[0, :, d * tok : (d + 2) * tok]
        else:
            right = jnp.concatenate([t_ref[0, :, d * tok :], jnp.zeros((2 * tok, tok), jnp.bfloat16)], axis=1)
        product = lax.dot_general(left, right, (((1,), (1,)), ((), ())), preferred_element_type=jnp.float32)
        term = product[:count, :tok] + (product[:count, tok:] + product[count:, :tok])
        if d == 0:
            grads[g] = term
        else:
            grads[g, :count, :] += term

    for d in range(0, used, 2):
        depth = min(rows, -(-(rows - d * per) // LANES) * LANES)
        high, low = [
            jnp.concatenate([ref[g, d * per : d * per + depth, :], ref[g, (d + 1) * per : (d + 1) * per + depth, :]], axis=1)
            for ref in (s_hi, s_lo)
        ]
        main = jnp.dot(left_ref[0, :, :depth], high, preferred_element_type=jnp.float32)
        rest = jnp.dot(left_ref[0, :tok, :depth], low, preferred_element_type=jnp.float32)
        stop = min(d + 2, steps)
        cross[:, d * tok : stop * tok] = (main[:tok] + (main[tok:] + rest))[:, : (stop - d) * tok]
    if used + used % 2 < steps:
        cross[:, (used + used % 2) * tok :] = jnp.zeros_like(cross[:, (used + used % 2) * tok :])
    skewed = pltpu.roll(cross[...], width - tok + 1, 1, stride=1, stride_axis=0)
    lag_sums[pl.ds(g, 1), :] = jnp.sum(skewed, axis=0, keepdims=True)[:, : width - tok] * scale

    @pl.when(g == groups - 1)
    def _():
        lags, lag_exponent = coded(lag_sums[...], largest(lag_sums[...]))
        held = out_ref.shape[1] - 8
        for a in range(blocks):
            out_ref[a, tok:held, :] = jnp.zeros_like(out_ref[a, tok:held, :])
            block = grads[:, a * per : (a + 1) * per, :].reshape(groups * per, tok).T
            code, exponent = coded(block, largest(block))
            if out_ref.shape[2] > groups * per:
                out_ref[a, :tok, :] = jnp.zeros_like(out_ref[a, :tok, :])
            out_ref[a, held:, :] = jnp.zeros_like(out_ref[a, held:, :])
            out_ref[a, :tok, : groups * per] = code
            out_ref[a, held : held + 1, : groups * per] = exponent
            own_lags = slice(a * lag_own, (a + 1) * lag_own)
            out_ref[a, tok : tok + groups, :lag_own] = lags[:, own_lags]
            out_ref[a, held + 1 : held + 2, :lag_own] = lag_exponent[:, own_lags]


def convolve(seq_blocks, input_blocks, moved, channels, lag_own, scale):
    blocks, tok, own = input_blocks.shape
    groups, _, width = moved.shape
    per = -(-channels // ROW_TILE) * ROW_TILE
    if groups * per != LANES or channels != per:
        wide = groups * per
        lanes = -(-wide // LANES) * LANES

        def widen(v):
            shape = v.shape[:-1]
            v = v.reshape(-1, groups, channels)
            v = jnp.pad(v, ((0, 0), (0, 0), (0, per - channels))).reshape(-1, wide)
            return jnp.pad(v, ((0, 0), (0, lanes - wide))).reshape(shape + (lanes,))

        seq_blocks, input_blocks = widen(seq_blocks), widen(input_blocks)
    rows = blocks * per
    left = stack_input(input_blocks, groups, per)
    extra = -(-(groups + 8) // ROW_TILE) * ROW_TILE
    out_lanes = max(groups * per, lag_own)
    return pl.pallas_call(
        functools.partial(conv_kernel, scale, lag_own),
        grid=(groups,),
        in_specs=[
            pl.BlockSpec(seq_blocks.shape, lambda g: (0, 0, 0)),
            pl.BlockSpec((1, 2 * tok, rows), lambda g: (g, 0, 0)),
            pl.BlockSpec((1, 2 * tok, width), lambda g: (g, 0, 0)),
        ],
        out_specs=pl.BlockSpec((blocks, tok + extra, out_lanes), lambda g: (0, 0, 0)),
        out_shape=jax.ShapeDtypeStruct((blocks, tok + extra, out_lanes), jnp.float32),
        scratch_shapes=[pltpu.VMEM((groups, 2 * rows, tok), jnp.bfloat16)] * 2
        + [
            pltpu.VMEM((groups, rows, tok), jnp.float32),
            pltpu.VMEM((tok, width), jnp.float32),
            pltpu.VMEM((groups, width - tok), jnp.float32),
        ],
        compiler_params=pltpu.CompilerParams(vmem_limit_bytes=48 * 1024 * 1024),
        cost_estimate=pl.CostEstimate(
            flops=groups * rows * tok * width * 14,
            bytes_accessed=12 * blocks * tok * LANES + 4 * groups * tok * width,
            transcendentals=0,
        ),
        name="convolve",
    )(seq_blocks, left, moved)


def nothing(*refs):
    del refs


def after(value, *earlier):
    return pl.pallas_call(
        nothing,
        in_specs=[ANY] * (1 + len(earlier)),
        out_specs=ANY,
        out_shape=jax.ShapeDtypeStruct(value.shape, value.dtype),
        input_output_aliases={0: 0},
        compiler_params=pltpu.CompilerParams(vmem_limit_bytes=1 * 1024 * 1024),
        cost_estimate=pl.CostEstimate(flops=0, bytes_accessed=0, transcendentals=0),
        name="after",
    )(value, *earlier)


class Place:
    def __init__(self):
        self.devices = lax.axis_size("ctx")
        self.ys = self.devices // 8
        assert self.devices == 8 * self.ys
        me = lax.axis_index("ctx")
        self.core, chip = lax.rem(me, 2), me // 2
        self.y, z = lax.rem(chip, self.ys), chip // self.ys
        self.p, self.h = lax.rem(z, 2), z // 2
        self.block = (self.h * self.ys + self.y) * 2 + self.core

    def index(self, h, p, y, core):
        return ((h * 2 + p) * self.ys + y) * 2 + core

    def all(self):
        return [(h, p, y, c) for h in range(2) for p in range(2) for y in range(self.ys) for c in range(2)]

    def swap_core(self, v):
        return lax.ppermute(v, "ctx", [(self.index(h, p, y, c), self.index(h, p, y, 1 - c)) for h, p, y, c in self.all()])

    def swap_pair(self, v):
        return lax.ppermute(v, "ctx", [(self.index(h, p, y, c), self.index(h, 1 - p, y, c)) for h, p, y, c in self.all()])

    def swap_half(self, v):
        return lax.ppermute(v, "ctx", [(self.index(h, p, y, c), self.index(1 - h, p, y, c)) for h, p, y, c in self.all()])

    def swap_half_and_pair(self, v):
        pairs = [(self.index(h, p, y, c), self.index(1 - h, 1 - p, y, c)) for h, p, y, c in self.all()]
        return lax.ppermute(v, "ctx", pairs)

    def along_y(self, v, shift):
        ys = self.ys
        return lax.ppermute(
            v, "ctx", [(self.index(h, p, y, c), self.index(h, p, (y + shift) % ys, c)) for h, p, y, c in self.all()]
        )

    def same_p(self):
        return [[self.index(h, p, y, c) for h in range(2) for y in range(self.ys) for c in range(2)] for p in range(2)]


def pick_kernel(features, slots, core_ref, *refs):
    parts, (mine_ref, theirs_ref) = refs[: 2 * slots], refs[-2:]
    tok, held = parts[0].shape
    first = core_ref[0] == 0
    for row in range(2):
        rows = slice(row * tok, (row + 1) * tok)
        for s in range(slots):
            part = parts[row * slots + s]
            for b in range(held // (2 * features)):
                even = part[:, 2 * b * features : (2 * b + 1) * features]
                odd = part[:, (2 * b + 1) * features : (2 * b + 2) * features]
                at = s * held // 2 + b * features
                mine_ref[rows, at : at + features] = jnp.where(first, even, odd)
                theirs_ref[rows, at : at + features] = jnp.where(first, odd, even)


def gather_cotangent(cotangent, features, place, earlier):
    tok, held = cotangent.shape
    parts = lax.axis_size("ch")
    far = place.swap_pair(cotangent)

    def along_ch(v):
        return [v] + [lax.ppermute(v, "ch", [(j, (j + s) % parts) for j in range(parts)]) for s in range(1, parts)]

    whole = jax.ShapeDtypeStruct((2 * tok, parts * held // 2), cotangent.dtype)
    mine, theirs = pl.pallas_call(
        functools.partial(pick_kernel, features, parts),
        in_specs=[SMEM] + [VMEM] * (2 * parts),
        out_specs=[VMEM] * 2,
        out_shape=[whole, whole],
        compiler_params=pltpu.CompilerParams(vmem_limit_bytes=10 * 1024 * 1024),
        cost_estimate=pl.CostEstimate(flops=0, bytes_accessed=8 * tok * held * parts, transcendentals=0),
        name="pick_features",
    )(place.core.reshape(1), *along_ch(cotangent), *along_ch(far))
    return mine, place.swap_core(after(theirs, *earlier))


def seq_kernel(p_ref, sum_ref, arrived_ref, gate_ref, far_gate_ref, *refs):
    out_ref, near_ref, far_ref = refs[-3:]
    p = p_ref[0]
    blocks, _, own = out_ref.shape
    tok = near_ref.shape[0]
    near_ref[...] = sum_ref[:tok, :] + arrived_ref[:tok, :]
    far_ref[...] = sum_ref[tok:, :] + arrived_ref[tok:, :]
    near = near_ref[...] * gate_ref[...]
    far = far_ref[...] * far_gate_ref[...]
    for b in range(blocks):
        here = slice(b * own, (b + 1) * own)
        most = jnp.maximum(largest(near[:, here]), largest(far[:, here]))
        for value, place in ((near, p), (far, 1 - p)):
            code, exponent = coded(value[:, here], most)
            out_ref[b, pl.ds(pl.multiple_of(place * tok, tok), tok), :] = code
        out_ref[b, 2 * tok :, :] = jnp.broadcast_to(exponent, (ROW_TILE, own))


def seq_blocks_of(total, arrived, gate_value, far_gate, place, *awaited):
    tok, channels = gate_value.shape
    blocks = place.devices // 2
    half = channels // 2
    own = half // blocks
    steps = max(1, min(4, half // LANES))
    width, count = half // steps, blocks // steps
    return pl.pallas_call(
        seq_kernel,
        grid_spec=pltpu.PrefetchScalarGridSpec(
            num_scalar_prefetch=1,
            grid=(steps,),
            in_specs=[
                pl.BlockSpec((2 * tok, width), lambda i, p: (0, i)),
                pl.BlockSpec((2 * tok, width), lambda i, p: (0, i)),
                pl.BlockSpec((tok, width), lambda i, p: (0, p[0] * steps + i)),
                pl.BlockSpec((tok, width), lambda i, p: (0, i)),
            ]
            + [ANY] * len(awaited),
            out_specs=[
                pl.BlockSpec((count, 2 * tok + ROW_TILE, own), lambda i, p: (i, 0, 0)),
                pl.BlockSpec((tok, width), lambda i, p: (0, i)),
                pl.BlockSpec((tok, width), lambda i, p: (0, i)),
            ],
        ),
        out_shape=[
            jax.ShapeDtypeStruct((blocks, 2 * tok + ROW_TILE, own), jnp.float32),
            pltpu.HBM((tok, half), jnp.float32),
            pltpu.HBM((tok, half), jnp.float32),
        ],
        compiler_params=pltpu.CompilerParams(vmem_limit_bytes=12 * 1024 * 1024),
        cost_estimate=pl.CostEstimate(
            flops=2 * tok * channels, bytes_accessed=24 * tok * channels, transcendentals=0
        ),
        name="seq_grad",
    )(place.p.reshape(1), total, arrived, gate_value, far_gate, *awaited)


def column_of(share, ctx, ch, ys, parts, features):
    other_h, other_p, shift = share
    chip = ctx // 2
    z, y = chip // ys, lax.rem(chip, ys)
    h, p = z // 2, lax.rem(z, 2)
    source = ((1 - h if other_h else h) * 2 + (1 - p if other_p else p)) * ys + lax.rem(y - shift + ys, ys)
    chips = 4 * ys // parts
    return (lax.rem(ch - source // chips + parts, parts) * chips + lax.rem(source, chips)) * features


def share_kernel(where, ys, parts, ctx_ref, ch_ref, mine_ref, theirs_ref, *refs):
    shares, before, (own_ref, other_ref) = refs[: len(where)], refs[len(where) : -2], refs[-2:]
    rows, features = mine_ref.shape[0], shares[0].shape[1]
    left = []
    for share in where:
        column = column_of(share, ctx_ref[0], ch_ref[0], ys, parts, features)
        at = pl.ds(pl.multiple_of(column, features), features)
        left.append(jnp.concatenate([mine_ref[:, at], theirs_ref[:, at]], axis=0))
    term = lax.dot_general(
        jnp.concatenate(left, axis=1),
        jnp.concatenate([share[...] for share in shares], axis=1),
        (((1,), (1,)), ((), ())),
        preferred_element_type=jnp.float32,
    )
    for i, ref in enumerate((own_ref, other_ref)):
        part = term[i * rows : (i + 1) * rows]
        ref[...] = part + before[i][...] if before else part


def add_shares(where, mine, theirs, shares, before, place):
    rows, (half, features) = mine.shape[0], shares[0].shape
    parts = lax.axis_size("ch")
    ctx, ch = lax.axis_index("ctx"), lax.axis_index("ch")
    if features % LANES:
        sums = list(before)
        for share, held in zip(where, shares):
            column = column_of(share, ctx, ch, place.ys, parts, features)
            terms = [
                lax.dot_general(
                    lax.dynamic_slice_in_dim(v, column, features, 1),
                    held,
                    (((1,), (1,)), ((), ())),
                    preferred_element_type=jnp.float32,
                )
                for v in (mine, theirs)
            ]
            sums = [a + b for a, b in zip(sums, terms)] if sums else terms
        return sums
    tile = min(512, half)
    whole = jax.ShapeDtypeStruct((rows, half), jnp.float32)
    tiles = pl.BlockSpec((rows, tile), lambda n: (0, n))
    return pl.pallas_call(
        functools.partial(share_kernel, where, place.ys, parts),
        grid=(half // tile,),
        in_specs=[SMEM] * 2
        + [pl.BlockSpec(mine.shape, lambda n: (0, 0))] * 2
        + [pl.BlockSpec((tile, features), lambda n: (n, 0))] * len(shares)
        + [tiles] * len(before),
        out_specs=[tiles] * 2,
        out_shape=[whole, whole],
        compiler_params=pltpu.CompilerParams(vmem_limit_bytes=GRANT),
        cost_estimate=pl.CostEstimate(
            flops=4 * rows * half * len(shares) * features,
            bytes_accessed=2 * (mine.size * 2 + half * len(shares) * features) + 16 * rows * half,
            transcendentals=0,
        ),
        name="add_shares",
    )(ctx.reshape(1), ch.reshape(1), mine, theirs, *shares, *before)


def project(cotangent, out_weight, place, waited, between):
    channels, features = out_weight.shape
    half = channels // 2
    near = lax.dynamic_slice_in_dim(out_weight, place.p * half, half, 0)
    given = lax.dynamic_slice_in_dim(out_weight, (1 - place.p) * half, half, 0)
    far = place.swap_half(near)
    paired = place.swap_pair(given)
    far_paired = place.swap_half_and_pair(after(given, far))

    def along_y(v):
        return [v] + [place.along_y(v, shift) for shift in range(1, place.ys)]

    held = [along_y(near)]
    held.append(along_y(after(paired, *held[0][1:])))
    held.append(along_y(far))
    held.append(along_y(after(far_paired, *held[1][1:], *held[2][1:])))
    made, sign = between(held[2][-1])
    mine, theirs = gather_cotangent(cotangent, features, place, [*held[3][1:], waited, sign])
    shares = [
        ((other // 2, other % 2, shift), held[other][shift]) for other in range(4) for shift in range(place.ys)
    ]
    sums = []
    for some in (shares,):
        sums = add_shares([at for at, _ in some], mine, theirs, [v for _, v in some], sums, place)
    own, other = sums
    return own, place.swap_core(other), made


def code_kernel(x_ref, *refs):
    out_ref = refs[-1]
    devices, rows, own = out_ref.shape
    tok = x_ref.shape[0]
    code, exponent = coded(x_ref[...], largest(x_ref[...]))
    quarter = devices // 4
    for i in range(devices):
        h, p, rest = i // (2 * quarter), i // quarter % 2, i % quarter
        block = (p * 2 + h) * quarter + rest
        out_ref[i, :tok, :] = code[:, block * own : (block + 1) * own]
        out_ref[i, tok:, :] = jnp.broadcast_to(exponent[:, block * own : (block + 1) * own], (rows - tok, own))


def code_blocks(value, devices, *awaited):
    tok, channels = value.shape
    return pl.pallas_call(
        code_kernel,
        in_specs=[VMEM] + [ANY] * len(awaited),
        out_specs=VMEM,
        out_shape=jax.ShapeDtypeStruct((devices, tok + ROW_TILE, channels // devices), jnp.float32),
        compiler_params=pltpu.CompilerParams(vmem_limit_bytes=8 * 1024 * 1024),
        cost_estimate=pl.CostEstimate(flops=4 * tok * channels, bytes_accessed=8 * tok * channels, transcendentals=0),
        name="code_input",
    )(value, *awaited)


def body(cotangent, out_weight, gate_value, conv_output, conv_input, filters):
    tok, channels = gate_value.shape
    all_groups, lags = filters.shape
    place = Place()
    devices = place.devices
    per_group = channels // all_groups
    own = channels // devices
    half = channels // 2
    groups = max(1, own // per_group)
    share = max(1, per_group // own)
    lag_own = lags // devices

    def exchange(blocks, groups=None):
        return lax.all_to_all(blocks, "ctx", 0, 0, tiled=True, axis_index_groups=groups)

    def reorder(blocks):
        return blocks.reshape((2, 2, devices // 4) + blocks.shape[1:]).swapaxes(0, 1).reshape(blocks.shape)

    far_gate = place.swap_pair(lax.dynamic_slice_in_dim(gate_value, (1 - place.p) * half, half, 1))

    def code_input(earlier):
        code = lax.optimization_barrier(code_blocks(conv_input, devices, earlier).astype(jnp.float16))
        return code, code[0, :8].astype(jnp.float32)

    total, arrived, code = project(cotangent, out_weight, place, far_gate, code_input)
    code = exchange(code)
    input_blocks = decoded(code[:, :tok], code[:, tok : tok + 1])
    first_group = (place.p * half + place.block * own) // per_group
    moved = toeplitz(lax.dynamic_slice_in_dim(filters, first_group, groups, 0), tok)

    seq_code, near, far = seq_blocks_of(total, arrived, gate_value, far_gate, place)
    seq_code = exchange(seq_code.astype(jnp.float16), place.same_p())
    seq_blocks = seq_code.astype(jnp.float32)
    far = place.swap_pair(far)
    left = jnp.where(place.p == 0, near, far)
    right = jnp.where(place.p == 0, far, near)
    gate_grad = jnp.concatenate([left, right], axis=1) * conv_output

    scale = 1.0 / math.sqrt(per_group * tok * devices)
    result = convolve(seq_blocks, input_blocks, moved, min(own, per_group), lag_own, scale)
    back = exchange(result[:, :, : max(own, lag_own)].astype(jnp.float16))
    held = back.shape[1] - 8
    input_grad = reorder(decoded(back[:, :tok, :own], back[:, held : held + 1, :own]))
    input_grad = input_grad.transpose(1, 0, 2).reshape(tok, channels)
    filter_grad = reorder(decoded(back[:, tok : tok + groups, :lag_own], back[:, held + 1 : held + 2, :lag_own]))
    filter_grad = filter_grad.reshape(all_groups, share, lag_own).sum(axis=1)
    return (input_grad, gate_grad, filter_grad)


def solution(mesh):
    return jax.shard_map(
        body,
        mesh=mesh,
        in_specs=(
            P("ctx", "ch"),
            P("ch", "ctx"),
            P("ctx", "ch"),
            P("ctx", "ch"),
            P("ctx", "ch"),
            P("ch", None),
        ),
        out_specs=(P("ctx", "ch"), P("ctx", "ch"), P("ch", "ctx")),
        check_vma=False,
    )
```
